32 devices in a mesh: pair: 4 (over y, x), mode: 8 (over z, core).
Axes of the slice: x: 2, y: 2, z: 4, core: 2. Of those that a mesh axis runs over, the one named last changes fastest.
Arguments:
- phi: bfloat16 [4, 384, 384, 384], P('pair', 'mode'), may hold values from -6 to 6
- eigvecs: bfloat16 [12, 384, 384], replicated, may hold values from -0.3125 to 0.3125
- freqs: float32 [12, 384], replicated, may hold values from 0.5 to 8
- occupations: float32 [12, 384], replicated, may hold values from 0.02 to 4
- smearing: float32 [12, 384], replicated, may hold values from 0.2 to 1
- probes: float32 [4, 2], P('pair'), may hold values from 0.5 to 8
- pair_index: int32 [4, 3], P('pair'), may hold values from 0 to 11
Outputs:
- sigma: float32 [384, 2, 384], P('mode', None, 'pair')
The draws below stay inside these ranges and needn't reach their ends.
All inputs are finite; a program needn't handle non-finite values.
Results may differ from the reference program's by a relative error of at most 0.0013.
Values may be sent and summed in bfloat16 or wider, within the bound.
No kernel may reach another device: no remote copies, remote signals or barrier semaphores. Data moves between devices by JAX's collectives and lax.ppermute only.
A program may use at most 128 MiB of HBM per device.

```python
import math
import jax
import jax.numpy as jnp
from jax import lax

M = 384
Q = 12
PAIRS = 4


def place_ends(values, key, least, high):
    longest = values.shape.index(max(values.shape))
    spots = []
    for shift in (0, 1):
        where = [jax.random.randint(jax.random.fold_in(key, axis), (), 0, length) for axis, length in enumerate(values.shape)]
        where[longest] = (where[longest] + shift) % values.shape[longest]
        spots.append(tuple(where))
    return values.at[spots[0]].set(least).at[spots[1]].set(high)


def shard_levels(rng, shape, cuts, least, high):
    def one(dim, parts):
        heights = jax.random.uniform(jax.random.fold_in(jax.random.fold_in(rng, 6), dim), (parts,), jnp.float32, least / len(cuts), high / len(cuts))
        return jnp.repeat(jnp.exp(heights), shape[dim] // parts).reshape((-1,) + (1,) * (len(shape) - dim - 1))

    gain = one(*cuts[0])
    for cut in cuts[1:]:
        gain = gain * one(*cut)
    return gain


def scatter_about(rng, extent, scale, most, split=(), held_as=jnp.bfloat16):
    array = jax.random.normal(rng, extent, jnp.float32) * scale
    if len(split) > 0:
        array = shard_levels(rng, extent, split, -0.22, 0.18) * array
    return jnp.clip(array, min=-most, max=most).astype(held_as)


def setup_inputs(seed: int = 0) -> dict:
    key_list = jax.random.split(jax.random.key(seed), 8)
    phi = scatter_about(key_list[0], (PAIRS, M, M, M), 1.0, 6.0, ((0, 4), (1, 8)))
    eigvecs = scatter_about(key_list[1], (Q, M, M), M ** -0.5, 0.3125)
    freqs = jnp.clip(jnp.exp(jax.random.uniform(key_list[2], (Q, M), jnp.float32, math.log(0.5), math.log(8.0))), 0.5, 8.0)
    occupations = jnp.clip(jnp.exp(jax.random.uniform(key_list[3], (Q, M), jnp.float32, math.log(0.02), math.log(4.0))), 0.02, 4.0)
    smearing = jnp.clip(jnp.exp(jax.random.uniform(key_list[4], (Q, M), jnp.float32, math.log(0.2), math.log(1.0))), 0.2, 1.0)
    probes = jnp.clip(0.5 + 7.5 * jax.random.uniform(key_list[5], (PAIRS, 2), jnp.float32) ** shard_levels(key_list[5], (PAIRS, 2), ((0, 4),), -0.2, 0.2), 0.5, 8.0)
    pair_index = place_ends(jax.random.randint(key_list[6], (PAIRS, 3), 0, Q), jax.random.fold_in(key_list[6], 1), 0, Q - 1).astype(jnp.int32)
    return dict(phi=phi, eigvecs=eigvecs, freqs=freqs, occupations=occupations, smearing=smearing, probes=probes, pair_index=pair_index)


def lorentz(offset, eta):
    return eta / (offset * offset + eta * eta)

def weights(f_one, n_one, h_one, f_two, n_two, h_two, omegas):
    total = f_two[:, None] + f_one[None, :]
    differ = f_two[:, None] - f_one[None, :]
    eta = 0.5 * (h_two[:, None] + h_one[None, :])
    bose_sum = 1.0 + n_one[None, :] + n_two[:, None]
    bose_diff = n_one[None, :] - n_two[:, None]
    result = []
    for probe in range(2):
        omega = omegas[probe]
        value = bose_sum * (lorentz(omega - total, eta) - lorentz(omega + total, eta))
        value = value + bose_diff * (lorentz(omega - differ, eta) - lorentz(omega + differ, eta))
        result.append(value)
    return jnp.stack(result)

def reference(phi, eigvecs, freqs, occupations, smearing, probes, pair_index):
    gram = jnp.zeros((M, 2, M), jnp.float32)
    for pidx in range(PAIRS):
        q_one = pair_index[pidx, 0]
        q_two = pair_index[pidx, 1]
        q_three = pair_index[pidx, 2]
        e_one = eigvecs[q_one]
        e_two = eigvecs[q_two]
        e_three = eigvecs[q_three]
        first = jnp.dot(phi[pidx].reshape(M * M, M), e_one, preferred_element_type=jnp.float32)
        first = first.astype(jnp.bfloat16).reshape(M, M, M)
        second = jnp.einsum('cbi,bj->cji', first.astype(jnp.float32), e_two.astype(jnp.float32))
        second = second.astype(jnp.bfloat16)
        rotated = lax.dot_general(e_three, second.reshape(M, M * M), (((0,), (0,)), ((), ())), preferred_element_type=jnp.float32).astype(jnp.bfloat16)
        wgt = weights(freqs[q_one], occupations[q_one], smearing[q_one], freqs[q_two], occupations[q_two], smearing[q_two], probes[pidx])
        for probe in range(2):
            weighted = (wgt[probe].reshape(1, M * M) * rotated.astype(jnp.float32)).astype(jnp.bfloat16)
            part = lax.dot_general(weighted, rotated, (((1,), (1,)), ((), ())), preferred_element_type=jnp.float32)
            gram = gram.at[:, probe, :].add(part)
    offdiag = (jnp.arange(M)[:, None] != jnp.arange(M)[None, :]).astype(jnp.float32)
    scale = 1.0 / (M * math.sqrt(PAIRS))
    return gram * offdiag[:, None, :] * scale
```

```python
import math

import jax
import jax.numpy as jnp
from jax import lax
from jax.experimental import pallas as pl
from jax.experimental.pallas import tpu as pltpu
from jax.sharding import PartitionSpec as P

LANES = 128
GROUP = 8
F32 = jnp.float32
BF16 = jnp.bfloat16


def lorentz(offset, eta):
    return eta / (offset * offset + eta * eta)


def weight_pair(f_one, n_one, h_one, f_two, n_two, h_two, omega):
    total = f_two + f_one
    differ = f_two - f_one
    eta = 0.5 * (h_two + h_one)
    value = (1.0 + n_one + n_two) * (lorentz(omega - total, eta) - lorentz(omega + total, eta))
    return value + (n_one - n_two) * (lorentz(omega - differ, eta) - lorentz(omega + differ, eta))


def rotate_kernel(phi_ref, one_ref, two_ref, out_ref, held, turned):
    block, rows, inner = phi_ref.shape
    cols = one_ref.shape[1]
    first = jnp.dot(phi_ref[...].reshape(block * rows, inner), one_ref[...], preferred_element_type=F32)
    first = first.astype(BF16)
    for c in range(block):
        held[:, c * cols : (c + 1) * cols] = first[c * rows : (c + 1) * rows]
    wide = jnp.dot(two_ref[...], held[...], preferred_element_type=F32)
    for c in range(block):
        turned[pl.ds(c, two_ref.shape[0], stride=block), :] = wide[:, c * cols : (c + 1) * cols]
    out_ref[...] = turned[...].reshape(two_ref.shape[0], block, cols).astype(BF16)


def rotate(phi, e_one, e_two_t, block):
    slices, rows, inner = phi.shape
    cols = e_one.shape[1]
    modes = e_two_t.shape[0]
    return pl.pallas_call(
        rotate_kernel,
        grid=(slices // block,),
        in_specs=[
            pl.BlockSpec((block, rows, inner), lambda g: (g, 0, 0)),
            pl.BlockSpec((inner, cols), lambda g: (0, 0)),
            pl.BlockSpec((modes, rows), lambda g: (0, 0)),
        ],
        out_specs=pl.BlockSpec((modes, block, cols), lambda g: (0, g, 0)),
        out_shape=jax.ShapeDtypeStruct((modes, slices, cols), BF16),
        scratch_shapes=[
            pltpu.VMEM((rows, block * cols), BF16),
            pltpu.VMEM((modes * block, cols), F32),
        ],
        compiler_params=pltpu.CompilerParams(vmem_limit_bytes=40 * 2**20),
        cost_estimate=pl.CostEstimate(
            flops=2 * slices * rows * inner * cols + 2 * slices * rows * cols * modes,
            bytes_accessed=slices * rows * inner * 2 + modes * slices * cols * 2,
            transcendentals=0,
        ),
        name="rotate",
    )(phi, e_one, e_two_t)


def gram_kernel(omegas, arr_ref, three_ref, row_ref, col_ref, old_ref, out_ref, side):
    sources, span, slices, cols = arr_ref.shape
    modes = three_ref.shape[0]
    step = pl.program_id(0)

    @pl.when(step == 0)
    def _():
        out_ref[...] = old_ref[...]

    weights = [[], []]
    for g in range(span):
        side[:, g * cols : (g + 1) * cols] = arr_ref[:, g].reshape(modes, cols)
        for w in range(2):
            weights[w].append(
                weight_pair(
                    row_ref[0:1, :], row_ref[1:2, :], row_ref[2:3, :],
                    col_ref[g : g + 1, 0:1], col_ref[g : g + 1, 1:2], col_ref[g : g + 1, 2:3],
                    omegas[0, w],
                )
            )
    rotated = jnp.dot(three_ref[...], side[...], preferred_element_type=F32).astype(BF16)
    wide = rotated.astype(F32)
    for w in range(2):
        scaled = (wide * jnp.concatenate(weights[w], axis=1)).astype(BF16)
        out_ref[w] += lax.dot_general(rotated, scaled, (((1,), (1,)), ((), ())), preferred_element_type=F32)


def gram(arrived, e_three_t, rows, cols, omegas, old, group):
    sources, span, slices, width = arrived.shape
    modes = e_three_t.shape[0]
    return pl.pallas_call(
        gram_kernel,
        grid=(span // group,),
        in_specs=[
            pl.BlockSpec(memory_space=pltpu.SMEM),
            pl.BlockSpec((sources, group, slices, width), lambda g: (0, g, 0, 0)),
            pl.BlockSpec((modes, modes), lambda g: (0, 0)),
            pl.BlockSpec((3, width), lambda g: (0, 0)),
            pl.BlockSpec((group, 3), lambda g: (g, 0)),
            pl.BlockSpec((2, modes, modes), lambda g: (0, 0, 0)),
        ],
        out_specs=pl.BlockSpec((2, modes, modes), lambda g: (0, 0, 0)),
        out_shape=jax.ShapeDtypeStruct((2, modes, modes), F32),
        scratch_shapes=[pltpu.VMEM((modes, group * width), BF16)],
        input_output_aliases={5: 0},
        compiler_params=pltpu.CompilerParams(vmem_limit_bytes=40 * 2**20),
        cost_estimate=pl.CostEstimate(
            flops=2 * modes * modes * span * width * 3,
            bytes_accessed=arrived.size * 2 + modes * modes * 16,
            transcendentals=0,
        ),
        name="gram",
    )(omegas, arrived, e_three_t, rows, cols, old)


def rotate_plain(phi, e_one, e_two_t):
    first = jnp.einsum("cba,ai->cbi", phi, e_one, preferred_element_type=F32).astype(BF16)
    return jnp.einsum("jb,cbi->jci", e_two_t, first, preferred_element_type=F32).astype(BF16)


def gram_plain(arrived, e_three_t, rows, cols, omegas, old):
    sources, span, slices, width = arrived.shape
    modes = e_three_t.shape[0]
    side = jnp.transpose(arrived, (0, 2, 1, 3)).reshape(modes, span * width)
    rotated = jnp.dot(e_three_t, side, preferred_element_type=F32).astype(BF16)
    for w in range(2):
        wgt = weight_pair(
            rows[0:1], rows[1:2], rows[2:3], cols[:, 0:1], cols[:, 1:2], cols[:, 2:3], omegas[0, w]
        ).reshape(1, span * width)
        scaled = (rotated.astype(F32) * wgt).astype(BF16)
        old = old.at[w].add(jnp.einsum("kl,nl->kn", rotated, scaled, preferred_element_type=F32))
    return old


def shards(phi, eigvecs, freqs, occupations, smearing, probes, pair_index):
    tensor = phi[0]
    slices, modes = tensor.shape[0], tensor.shape[1]
    pairs, parts = lax.axis_size("pair"), lax.axis_size("mode")
    span = modes // parts
    q_one, q_two, q_three = pair_index[0, 0], pair_index[0, 1], pair_index[0, 2]
    pick = lambda table, q: lax.dynamic_index_in_dim(table, q, 0, keepdims=False)
    e_one = pick(eigvecs, q_one)
    e_two_t = pick(eigvecs, q_two).T
    e_three_t = pick(eigvecs, q_three).T
    rows = jnp.stack([pick(freqs, q_one), pick(occupations, q_one), pick(smearing, q_one)])
    cols = jnp.stack([pick(freqs, q_two), pick(occupations, q_two), pick(smearing, q_two)])
    place = lax.axis_index("mode")
    cols = lax.dynamic_slice_in_dim(cols, place * span, span, axis=1).T
    tiled = slices % 16 == 0 and span % GROUP == 0
    total = jnp.zeros((2, modes, modes), F32)
    for start in range(0, modes, LANES):
        block = e_one[:, start : start + LANES]
        width = block.shape[1]
        if tiled:
            second = rotate(tensor, block, e_two_t, 16)
        else:
            second = rotate_plain(tensor, block, e_two_t)
        second = second.reshape(parts, span, slices, width)
        arrived = lax.all_to_all(second, "mode", split_axis=0, concat_axis=0, tiled=True)
        head = rows[:, start : start + LANES]
        if tiled:
            total = gram(arrived, e_three_t, head, cols, probes, total, GROUP)
        else:
            total = gram_plain(arrived, e_three_t, head, cols, probes, total)
    core = place % 2
    kept = lax.dynamic_index_in_dim(total, core, 0, keepdims=False)
    given = lax.dynamic_index_in_dim(total, 1 - core, 0, keepdims=False)
    swap = [(i, i ^ 1) for i in range(parts)]
    part = kept + lax.ppermute(given, "mode", swap)
    part = part.reshape(pairs, modes // pairs, modes)
    low, high = part[:, : modes // pairs // 2], part[:, modes // pairs // 2 :]
    distances = [1 << b for b in range(pairs.bit_length() - 1)]
    low = halvings(low, "pair", pairs, distances)
    high = halvings(high, "pair", pairs, distances[::-1])
    part = jnp.concatenate([low[0], high[0]], axis=0).T
    part = part.reshape(parts // 2, 2, span, modes // pairs)
    part = halvings(part, "mode", parts, [2 << b for b in range(parts.bit_length() - 2)])[0]
    kept = lax.dynamic_index_in_dim(part, core, 0, keepdims=False)
    given = lax.dynamic_index_in_dim(part, 1 - core, 0, keepdims=False)
    taken = lax.ppermute(given, "mode", swap)
    local = jnp.stack([jnp.where(core == 0, kept, taken), jnp.where(core == 0, taken, kept)], axis=1)
    row_ids = place * span + jnp.arange(span, dtype=jnp.int32)
    count = modes // pairs
    col_ids = lax.axis_index("pair") * count + jnp.arange(count, dtype=jnp.int32)
    offdiag = (row_ids[:, None] != col_ids[None, :]).astype(F32)
    scale = 1.0 / (modes * math.sqrt(pairs))
    return local * offdiag[:, None, :] * scale


def halvings(x, axis, size, distances):
    place = lax.axis_index(axis)
    low = distances and min(distances)
    bits = [d // low for d in distances]
    left = list(bits)
    for distance, unit in zip(distances, bits):
        order = sorted(left, reverse=True)
        at = order.index(unit)
        outer, inner = 1 << at, 1 << (len(order) - at - 1)
        view = x.reshape(outer, 2, inner, *x.shape[1:])
        bit = (place // distance) % 2
        mine = lax.dynamic_index_in_dim(view, bit, 1, keepdims=False)
        other = lax.dynamic_index_in_dim(view, 1 - bit, 1, keepdims=False)
        got = lax.ppermute(other, axis, [(i, i ^ distance) for i in range(size)])
        x = (mine + got).reshape(outer * inner, *x.shape[1:])
        left.remove(unit)
    return x


def solution(mesh):
    return jax.shard_map(
        shards,
        mesh=mesh,
        in_specs=(
            P("pair", "mode", None, None),
            P(),
            P(),
            P(),
            P(),
            P("pair", None),
            P("pair", None),
        ),
        out_specs=P("mode", None, "pair"),
        check_vma=False,
    )
```

```python
import functools
import math

import jax
import jax.numpy as jnp
from jax import lax
from jax.experimental import pallas as pl
from jax.experimental.pallas import tpu as pltpu
from jax.sharding import PartitionSpec as P

F32 = jnp.float32
BF16 = jnp.bfloat16
LANES = 128
ROWS = 16
VMEM = 48 * 2**20


def lorentz(offset, eta):
    return eta / (offset * offset + eta * eta)


def weights(f_one, n_one, h_one, f_two, n_two, h_two, omegas):
    total = f_two[:, None] + f_one[None, :]
    differ = f_two[:, None] - f_one[None, :]
    eta = 0.5 * (h_two[:, None] + h_one[None, :])
    bose_sum = 1.0 + n_one[None, :] + n_two[:, None]
    bose_diff = n_one[None, :] - n_two[:, None]
    result = []
    for probe in range(2):
        omega = omegas[probe]
        value = bose_sum * (lorentz(omega - total, eta) - lorentz(omega + total, eta))
        value = value + bose_diff * (lorentz(omega - differ, eta) - lorentz(omega + differ, eta))
        result.append(value)
    return jnp.stack(result)


def weight_pair(f_one, n_one, h_one, f_two, n_two, h_two, omega):
    total = f_two + f_one
    differ = f_two - f_one
    eta = 0.5 * (h_two + h_one)
    value = (1.0 + n_one + n_two) * (lorentz(omega - total, eta) - lorentz(omega + total, eta))
    return value + (n_one - n_two) * (lorentz(omega - differ, eta) - lorentz(omega + differ, eta))


def rotate_kernel(parts, span, j_low, index, phi_ref, one_ref, two_ref, *rest):
    outs, (turned_two, picked, held, turned) = rest[:parts], rest[parts:]
    j_count = outs[0].shape[0]
    _, block, rows, inner = phi_ref.shape
    cols = one_ref.shape[2]
    place = lax.axis_index("mode")

    @pl.when(pl.program_id(0) == 0)
    def _():
        turned_two[...] = two_ref[0].T
        for s in range(parts):
            low = pl.multiple_of((place ^ s) * span + j_low, ROWS)
            picked[s * j_count : (s + 1) * j_count] = turned_two[pl.ds(low, j_count)]

    first = jnp.dot(phi_ref[0].reshape(block * rows, inner), one_ref[0], preferred_element_type=F32)
    first = first.astype(BF16)
    for c in range(block):
        held[:, c * cols : (c + 1) * cols] = first[c * rows : (c + 1) * rows]
    wide = jnp.dot(picked[...], held[...], preferred_element_type=F32)
    for c in range(block):
        turned[pl.ds(c, parts * j_count, stride=block), :] = wide[:, c * cols : (c + 1) * cols]
    size = j_count * block
    for s in range(parts):
        outs[s][...] = turned[s * size : (s + 1) * size].reshape(j_count, block, cols).astype(BF16)


def rotate(phi, eigvecs, pair_index, parts, tile, c_low, c_count, j_low, j_count):
    _, slices, rows, inner = phi.shape
    modes = eigvecs.shape[2]
    first_block = c_low // ROWS
    flops = 2 * c_count * rows * LANES * (inner + parts * j_count)
    return pl.pallas_call(
        functools.partial(rotate_kernel, parts, modes // parts, j_low),
        grid_spec=pltpu.PrefetchScalarGridSpec(
            num_scalar_prefetch=1,
            grid=(c_count // ROWS,),
            in_specs=[
                pl.BlockSpec((1, ROWS, rows, inner), lambda g, index: (0, first_block + g, 0, 0)),
                pl.BlockSpec((1, inner, LANES), lambda g, index: (index[0, 0], 0, tile)),
                pl.BlockSpec((1, rows, modes), lambda g, index: (index[0, 1], 0, 0)),
            ],
            out_specs=[pl.BlockSpec((j_count, ROWS, LANES), lambda g, index: (0, g, 0))] * parts,
            scratch_shapes=[
                pltpu.VMEM((modes, rows), BF16),
                pltpu.VMEM((parts * j_count, rows), BF16),
                pltpu.VMEM((rows, ROWS * LANES), BF16),
                pltpu.VMEM((parts * j_count * ROWS, LANES), F32),
            ],
        ),
        out_shape=[jax.ShapeDtypeStruct((j_count, c_count, LANES), BF16)] * parts,
        compiler_params=pltpu.CompilerParams(vmem_limit_bytes=VMEM),
        cost_estimate=pl.CostEstimate(
            flops=flops,
            bytes_accessed=2 * c_count * (rows * inner + parts * j_count * LANES),
            transcendentals=0,
        ),
        name="rotate",
    )(pair_index, phi, eigvecs, eigvecs)


def gram_kernel(parts, c_counts, fresh, omegas, three_ref, row_ref, col_ref, *rest):
    pieces = len(c_counts)
    arrived, rest = rest[: parts * pieces], rest[parts * pieces :]
    old, (keep_ref, give_ref, side, rotated) = ((), rest) if fresh else (rest[:2], rest[2:])
    modes = three_ref.shape[0]
    slices = sum(c_counts)
    group, _, cols = arrived[0].shape
    half = modes // 2
    span = modes // parts
    core = lax.axis_index("mode") % 2

    @pl.when(pl.program_id(0) == 0)
    def _():
        for at, ref in enumerate((keep_ref, give_ref)):
            ref[...] = jnp.zeros_like(ref) if fresh else old[at][...]

    for g in range(group):
        for s in range(parts):
            low = s * slices
            for piece, count in enumerate(c_counts):
                side[low : low + count, g * cols : (g + 1) * cols] = arrived[s * pieces + piece][g]
                low += count
    rotated[...] = jnp.dot(three_ref[...], side[...], preferred_element_type=F32).astype(BF16)
    blocks = []
    for order in (core, 1 - core):
        for z in range(parts // 2):
            low = pl.multiple_of((2 * z + order) * span, ROWS)
            blocks.append(rotated[pl.ds(low, span)])
    ordered = jnp.concatenate(blocks, axis=0).astype(F32)
    for w in range(2):
        weights = [
            weight_pair(
                row_ref[0:1, :], row_ref[1:2, :], row_ref[2:3, :],
                col_ref[g : g + 1, 0:1], col_ref[g : g + 1, 1:2], col_ref[g : g + 1, 2:3],
                omegas[0, w],
            )
            for g in range(group)
        ]
        scaled = (ordered * jnp.concatenate(weights, axis=1)).astype(BF16)
        sums = lax.dot_general(
            scaled, rotated[...], (((1,), (1,)), ((), ())), preferred_element_type=F32
        )
        keep_ref[w] += sums[:half]
        give_ref[w] += sums[half:]


def gram(arrived, c_counts, three, rows, cols, probes, old, tile, j_low, group):
    parts = len(arrived)
    pieces = [piece for one in arrived for piece in one]
    j_count = pieces[0].shape[0]
    modes = three.shape[0]
    half = modes // 2
    fresh = old is None
    whole = pl.BlockSpec((2, half, modes), lambda g: (0, 0, 0))
    return pl.pallas_call(
        functools.partial(gram_kernel, parts, c_counts, fresh),
        grid=(j_count // group,),
        in_specs=[
            pl.BlockSpec(memory_space=pltpu.SMEM),
            pl.BlockSpec((modes, modes), lambda g: (0, 0)),
            pl.BlockSpec((3, LANES), lambda g: (0, tile)),
            pl.BlockSpec((group, 3), lambda g: (j_low // group + g, 0)),
        ]
        + [pl.BlockSpec((group, p.shape[1], LANES), lambda g: (g, 0, 0)) for p in pieces]
        + ([] if fresh else [whole, whole]),
        out_specs=[whole, whole],
        out_shape=[jax.ShapeDtypeStruct((2, half, modes), F32)] * 2,
        scratch_shapes=[
            pltpu.VMEM((modes, group * LANES), BF16),
            pltpu.VMEM((modes, group * LANES), BF16),
        ],
        input_output_aliases={} if fresh else {4 + len(pieces): 0, 5 + len(pieces): 1},
        compiler_params=pltpu.CompilerParams(vmem_limit_bytes=VMEM),
        cost_estimate=pl.CostEstimate(
            flops=6 * modes * modes * j_count * LANES,
            bytes_accessed=2 * modes * j_count * LANES + 16 * modes * modes,
            transcendentals=0,
        ),
        name="gram",
    )(probes, three, rows, cols, *pieces, *(() if fresh else old))


def to_pairs_kernel(keep_ref, got_ref, *rest):
    outs, turned = rest[:-1], rest[-1]
    count = outs[0].shape[0]
    modes = turned.shape[0]
    turned[...] = (keep_ref[...] + got_ref[...]).reshape(modes, modes).T
    place = lax.axis_index("pair")
    for s, out in enumerate(outs):
        out[...] = turned[pl.ds(pl.multiple_of((place ^ s) * count, 8), count)]


def to_pairs(keep, got, pairs):
    modes = keep.shape[2]
    return pl.pallas_call(
        to_pairs_kernel,
        out_shape=[jax.ShapeDtypeStruct((modes // pairs, modes), F32)] * pairs,
        scratch_shapes=[pltpu.VMEM((modes, modes), F32)],
        compiler_params=pltpu.CompilerParams(vmem_limit_bytes=VMEM),
        name="to_pairs",
    )(keep, got)


def to_modes_kernel(chips, *rest):
    parts, outs, turned = rest[: -chips - 1], rest[-chips - 1 : -1], rest[-1]
    _, span, count = outs[0].shape
    turned[...] = sum(part[...] for part in parts).T
    half = turned.shape[0] // 2
    place = lax.axis_index("mode") // 2
    for s, out in enumerate(outs):
        low = pl.multiple_of((place ^ s) * span, 8)
        out[0] = turned[pl.ds(low, span)]
        out[1] = turned[pl.ds(half + low, span)]


def to_modes(parts, chips):
    count, modes = parts[0].shape
    span = modes // 2 // chips
    return pl.pallas_call(
        functools.partial(to_modes_kernel, chips),
        out_shape=[jax.ShapeDtypeStruct((2, span, count), F32)] * chips,
        scratch_shapes=[pltpu.VMEM((modes, count), F32)],
        compiler_params=pltpu.CompilerParams(vmem_limit_bytes=VMEM),
        name="to_modes",
    )(*parts)


def swap(x, axis, size, distance):
    return lax.ppermute(x, axis, [(i, i ^ distance) for i in range(size)])


def plan(modes, slices, span):
    whole = [(0, slices)]
    cuts = [(0, ROWS), (ROWS, slices - ROWS)] if slices > ROWS else whole
    blocks = [(0, cuts, 0, ROWS)]
    if span > ROWS:
        blocks.append((0, whole, ROWS, span - ROWS))
    for tile in range(1, modes // LANES):
        if tile == modes // LANES - 1 and span > ROWS:
            blocks.append((tile, whole, 0, span - ROWS))
            blocks.append((tile, whole, span - ROWS, ROWS))
        else:
            blocks.append((tile, whole, 0, span))
    return blocks


def shards(phi, eigvecs, freqs, occupations, smearing, probes, pair_index):
    _, slices, modes, _ = phi.shape
    pairs, parts = lax.axis_size("pair"), lax.axis_size("mode")
    span = modes // parts
    place = lax.axis_index("mode")
    others = lax.iota(jnp.int32, parts) ^ place

    def pick(table, at):
        return lax.dynamic_index_in_dim(table, pair_index[0, at], 0, keepdims=False)

    three = pick(eigvecs, 2).reshape(parts, slices, modes)[others].reshape(modes, modes).T
    rows = jnp.stack([pick(freqs, 0), pick(occupations, 0), pick(smearing, 0)])
    cols = jnp.stack([pick(freqs, 1), pick(occupations, 1), pick(smearing, 1)])
    cols = lax.dynamic_slice_in_dim(cols, place * span, span, axis=1).T
    blocks = plan(modes, slices, span)

    def turn(step, after):
        tile, cuts, j_low, j_count = blocks[step]
        if after is None:
            tensor = phi
        else:
            tensor, _ = lax.optimization_barrier((phi, after))
        return [
            rotate(tensor, eigvecs, pair_index, parts, tile, c_low, c_count, j_low, j_count)
            for c_low, c_count in cuts
        ]

    far = list(range(parts // 2, parts))
    near = list(range(1, parts // 2))
    sums, before = None, None
    ready = [turn(0, None), turn(1, None)]
    for step, (tile, cuts, j_low, j_count) in enumerate(blocks):
        arrived = [[] for _ in range(parts)]
        arrived[0] = [piece[0] for piece in ready[step]]
        for s in far + near:
            for piece in ready[step]:
                block = piece[s]
                if before is not None:
                    block, _ = lax.optimization_barrier((block, before[s][-1]))
                arrived[s].append(swap(block, "mode", parts, s))
        if step + 2 < len(blocks):
            ready.append(turn(step + 2, [arrived[s][-1] for s in far]))
        counts = [count for _, count in cuts]
        sums = gram(arrived, counts, three, rows, cols, probes, sums, tile, j_low, 8)
        before = arrived
    keep, give = sums
    blocks = to_pairs(keep, swap(give, "mode", parts, 1), pairs)
    blocks = [b if s == 0 else swap(b, "pair", pairs, s) for s, b in enumerate(blocks)]
    blocks = to_modes(blocks, parts // 2)
    blocks = [b if s == 0 else swap(b, "mode", parts, 2 * s) for s, b in enumerate(blocks)]
    local = jnp.transpose(sum(blocks), (1, 0, 2))
    row_count, _, col_count = local.shape
    row_ids = place * row_count + jnp.arange(row_count, dtype=jnp.int32)
    col_ids = lax.axis_index("pair") * col_count + jnp.arange(col_count, dtype=jnp.int32)
    offdiag = (row_ids[:, None] != col_ids[None, :]).astype(F32)
    scale = 1.0 / (modes * math.sqrt(pairs))
    return local * offdiag[:, None, :] * scale


def shards_plain(phi, eigvecs, freqs, occupations, smearing, probes, pair_index):
    tensor = phi[0]
    slices = tensor.shape[0]
    modes = tensor.shape[1]
    q_one = pair_index[0, 0]
    q_two = pair_index[0, 1]
    q_three = pair_index[0, 2]
    e_one = lax.dynamic_index_in_dim(eigvecs, q_one, 0, keepdims=False)
    e_two = lax.dynamic_index_in_dim(eigvecs, q_two, 0, keepdims=False)
    e_three = lax.dynamic_index_in_dim(eigvecs, q_three, 0, keepdims=False)
    first = jnp.dot(
        tensor.reshape(slices * modes, modes), e_one, preferred_element_type=jnp.float32
    )
    first = first.astype(jnp.bfloat16).reshape(slices, modes, modes)
    second = jnp.einsum("cbi,bj->cji", first, e_two, preferred_element_type=jnp.float32).astype(
        jnp.bfloat16
    )
    arrived = lax.all_to_all(second, "mode", split_axis=1, concat_axis=0, tiled=True)
    span = arrived.shape[1]
    count = arrived.shape[2]
    flat = lax.dot_general(
        e_three,
        arrived.reshape(arrived.shape[0], span * count),
        (((0,), (0,)), ((), ())),
        preferred_element_type=jnp.float32,
    )
    rotated = flat.astype(jnp.bfloat16).reshape(modes, span, count)
    span = rotated.shape[1]
    offset = lax.axis_index("mode") * span
    f_two = lax.dynamic_slice_in_dim(freqs[q_two], offset, span)
    n_two = lax.dynamic_slice_in_dim(occupations[q_two], offset, span)
    h_two = lax.dynamic_slice_in_dim(smearing[q_two], offset, span)
    wgt = weights(freqs[q_one], occupations[q_one], smearing[q_one], f_two, n_two, h_two, probes[0])
    flat_rot = rotated.reshape(modes, span * modes)
    weighted = (wgt.reshape(2, 1, span * modes) * flat_rot.astype(jnp.float32)[None]).astype(
        jnp.bfloat16
    )
    pair_size = lax.axis_size("pair")
    whole = jnp.einsum("wkl,nl->kwn", weighted, flat_rot, preferred_element_type=jnp.float32)
    reduced = lax.psum_scatter(whole, "pair", scatter_dimension=2, tiled=True)
    local = lax.psum_scatter(reduced, "mode", scatter_dimension=0, tiled=True)
    row_count = local.shape[0]
    col_count = local.shape[2]
    row_ids = lax.axis_index("mode") * row_count + jnp.arange(row_count, dtype=jnp.int32)
    col_ids = lax.axis_index("pair") * col_count + jnp.arange(col_count, dtype=jnp.int32)
    offdiag = (row_ids[:, None] != col_ids[None, :]).astype(jnp.float32)
    scale = 1.0 / (modes * math.sqrt(pair_size))
    return local * offdiag[:, None, :] * scale


def solution(mesh):
    pairs, parts = mesh.shape["pair"], mesh.shape["mode"]

    def either(phi, *rest):
        _, slices, modes, _ = phi.shape
        fits = slices % ROWS == 0 and modes % LANES == 0 and slices * parts == modes
        fits = fits and parts > 1 and parts & (parts - 1) == 0 and pairs & (pairs - 1) == 0
        fits = fits and modes % (8 * pairs) == 0
        return (shards if fits else shards_plain)(phi, *rest)

    return jax.shard_map(
        either,
        mesh=mesh,
        in_specs=(
            P("pair", "mode", None, None),
            P(),
            P(),
            P(),
            P(),
            P("pair", None),
            P("pair", None),
        ),
        out_specs=P("mode", None, "pair"),
        check_vma=False,
    )
```

```python
import functools
import math

import jax
import jax.numpy as jnp
from jax import lax
from jax.experimental import pallas as pl
from jax.experimental.pallas import tpu as pltpu
from jax.sharding import PartitionSpec as P

F32 = jnp.float32
BF16 = jnp.bfloat16
LANES = 128
ROWS = 16
VMEM = 60 * 2**20


def lorentz(offset, eta):
    return eta / (offset * offset + eta * eta)


def weights(f_one, n_one, h_one, f_two, n_two, h_two, omegas):
    total = f_two[:, None] + f_one[None, :]
    differ = f_two[:, None] - f_one[None, :]
    eta = 0.5 * (h_two[:, None] + h_one[None, :])
    bose_sum = 1.0 + n_one[None, :] + n_two[:, None]
    bose_diff = n_one[None, :] - n_two[:, None]
    result = []
    for probe in range(2):
        omega = omegas[probe]
        value = bose_sum * (lorentz(omega - total, eta) - lorentz(omega + total, eta))
        value = value + bose_diff * (lorentz(omega - differ, eta) - lorentz(omega + differ, eta))
        result.append(value)
    return jnp.stack(result)


def weight_pair(f_one, n_one, h_one, f_two, n_two, h_two, omega):
    total = f_two + f_one
    differ = f_two - f_one
    eta = 0.5 * (h_two + h_one)
    value = (1.0 + n_one + n_two) * (lorentz(omega - total, eta) - lorentz(omega + total, eta))
    return value + (n_one - n_two) * (lorentz(omega - differ, eta) - lorentz(omega + differ, eta))


def rotate_kernel(parts, span, j_cuts, index, phi_ref, one_ref, two_ref, *rest):
    outs, (turned_two, picked, held, turned) = rest[:-4], rest[-4:]
    j_low, j_count = j_cuts[0][0], sum(count for _, count in j_cuts)
    _, block, rows, inner = phi_ref.shape
    cols = one_ref.shape[2]
    place = lax.axis_index("mode")
    step = pl.program_id(0)

    @pl.when(step == 0)
    def _():
        turned_two[...] = two_ref[0].T
        for s in range(parts):
            low = pl.multiple_of((place ^ s) * span + j_low, ROWS)
            picked[s * j_count : (s + 1) * j_count] = turned_two[pl.ds(low, j_count)]

    first = jnp.dot(phi_ref[0].reshape(block * rows, inner), one_ref[0], preferred_element_type=F32)
    first = first.astype(BF16)
    for c in range(block):
        held[:, c * cols : (c + 1) * cols] = first[c * rows : (c + 1) * rows]
    wide = jnp.dot(picked[...], held[...], preferred_element_type=F32)
    at = lax.rem(step * block, ROWS)
    for c in range(block):
        turned[pl.ds(at + c, parts * j_count, stride=ROWS), :] = wide[:, c * cols : (c + 1) * cols]

    @pl.when(at == ROWS - block)
    def _():
        for cut, (low, count) in enumerate(j_cuts):
            for s in range(parts):
                start = (s * j_count + low - j_low) * ROWS
                piece = turned[start : start + count * ROWS].reshape(count, ROWS, cols)
                outs[cut * parts + s][...] = piece.astype(BF16)


def rotate(phi, eigvecs, pair_index, parts, tile, c_low, c_count, j_cuts, step):
    _, _, rows, inner = phi.shape
    modes = eigvecs.shape[2]
    j_count = sum(count for _, count in j_cuts)
    first_block = c_low // step
    outs = pl.pallas_call(
        functools.partial(rotate_kernel, parts, modes // parts, j_cuts),
        grid_spec=pltpu.PrefetchScalarGridSpec(
            num_scalar_prefetch=1,
            grid=(c_count // step,),
            in_specs=[
                pl.BlockSpec((1, step, rows, inner), lambda g, index: (0, first_block + g, 0, 0)),
                pl.BlockSpec((1, inner, LANES), lambda g, index: (index[0, 0], 0, tile)),
                pl.BlockSpec((1, rows, modes), lambda g, index: (index[0, 1], 0, 0)),
            ],
            out_specs=[
                pl.BlockSpec((count, ROWS, LANES), lambda g, index: (0, g * step // ROWS, 0))
                for _, count in j_cuts
                for _ in range(parts)
            ],
            scratch_shapes=[
                pltpu.VMEM((modes, rows), BF16),
                pltpu.VMEM((parts * j_count, rows), BF16),
                pltpu.VMEM((rows, step * LANES), BF16),
                pltpu.VMEM((parts * j_count * ROWS, LANES), F32),
            ],
        ),
        out_shape=[
            jax.ShapeDtypeStruct((count, c_count, LANES), BF16)
            for _, count in j_cuts
            for _ in range(parts)
        ],
        compiler_params=pltpu.CompilerParams(vmem_limit_bytes=VMEM),
        cost_estimate=pl.CostEstimate(flops=1, bytes_accessed=1, transcendentals=0),
        name="rotate",
    )(pair_index, phi, eigvecs, eigvecs)
    return [outs[cut * parts : (cut + 1) * parts] for cut in range(len(j_cuts))]


def gram_kernel(parts, c_counts, fresh, omegas, three_ref, row_ref, col_ref, *rest):
    pieces = len(c_counts)
    arrived, rest = rest[: parts * pieces], rest[parts * pieces :]
    old, (keep_ref, give_ref, side, rotated) = ((), rest) if fresh else (rest[:2], rest[2:])
    modes = three_ref.shape[0]
    slices = sum(c_counts)
    group, _, cols = arrived[0].shape
    half = modes // 2
    span = modes // parts
    core = lax.axis_index("mode") % 2

    @pl.when(pl.program_id(0) == 0)
    def _():
        for at, ref in enumerate((keep_ref, give_ref)):
            ref[...] = jnp.zeros_like(ref) if fresh else old[at][...]

    for g in range(group):
        for s in range(parts):
            low = s * slices
            for piece, count in enumerate(c_counts):
                side[low : low + count, g * cols : (g + 1) * cols] = arrived[s * pieces + piece][g]
                low += count
    rotated[...] = jnp.dot(three_ref[...], side[...], preferred_element_type=F32).astype(BF16)
    blocks = []
    for order in (core, 1 - core):
        for z in range(parts // 2):
            low = pl.multiple_of((2 * z + order) * span, ROWS)
            blocks.append(rotated[pl.ds(low, span)])
    ordered = jnp.concatenate(blocks, axis=0).astype(F32)
    scaled = []
    for w in range(2):
        weights = weight_pair(
            row_ref[0:1, :], row_ref[1:2, :], row_ref[2:3, :],
            col_ref[:, 0:1], col_ref[:, 1:2], col_ref[:, 2:3],
            omegas[0, w],
        )
        wide = jnp.concatenate([weights[g : g + 1] for g in range(group)], axis=1)
        scaled.append((ordered * wide).astype(BF16))
    sums = lax.dot_general(
        jnp.concatenate(scaled, axis=0),
        rotated[...],
        (((1,), (1,)), ((), ())),
        preferred_element_type=F32,
    )
    for w in range(2):
        keep_ref[w] += sums[2 * w * half : (2 * w + 1) * half]
        give_ref[w] += sums[(2 * w + 1) * half : (2 * w + 2) * half]


def gram(arrived, offsets, three, rows, cols, probes, old, tile, j_low, j_count, group):
    parts = len(arrived)
    pieces = [piece for one in arrived for piece in one]
    c_counts = [piece.shape[1] for piece in arrived[0]]
    blocks = [offset // group for offset in offsets] * parts
    modes = three.shape[0]
    half = modes // 2
    fresh = old is None
    whole = pl.BlockSpec((2, half, modes), lambda g: (0, 0, 0))
    return pl.pallas_call(
        functools.partial(gram_kernel, parts, c_counts, fresh),
        grid=(j_count // group,),
        in_specs=[
            pl.BlockSpec(memory_space=pltpu.SMEM),
            pl.BlockSpec((modes, modes), lambda g: (0, 0)),
            pl.BlockSpec((3, LANES), lambda g: (0, tile)),
            pl.BlockSpec((group, 3), lambda g: (j_low // group + g, 0)),
        ]
        + [
            pl.BlockSpec((group, p.shape[1], LANES), lambda g, b=b: (b + g, 0, 0))
            for p, b in zip(pieces, blocks)
        ]
        + ([] if fresh else [whole, whole]),
        out_specs=[whole, whole],
        out_shape=[jax.ShapeDtypeStruct((2, half, modes), F32)] * 2,
        scratch_shapes=[
            pltpu.VMEM((modes, group * LANES), BF16),
            pltpu.VMEM((modes, group * LANES), BF16),
        ],
        input_output_aliases={} if fresh else {4 + len(pieces): 0, 5 + len(pieces): 1},
        compiler_params=pltpu.CompilerParams(vmem_limit_bytes=VMEM // 2),
        cost_estimate=pl.CostEstimate(
            flops=int(1 * 6 * modes * modes * j_count * LANES),
            bytes_accessed=int(1 * (2 * modes * j_count * LANES + 16 * modes * modes)),
            transcendentals=0,
        ),
        name="gram",
    )(probes, three, rows, cols, *pieces, *(() if fresh else old))


def to_pairs_kernel(keep_ref, got_ref, *rest):
    outs, turned = rest[:-1], rest[-1]
    count = outs[0].shape[0]
    modes = turned.shape[0]
    turned[...] = (keep_ref[...] + got_ref[...]).reshape(modes, modes).T
    place = lax.axis_index("pair")
    for s, out in enumerate(outs):
        out[...] = turned[pl.ds(pl.multiple_of((place ^ s) * count, 8), count)]


def to_pairs(keep, got, pairs):
    modes = keep.shape[2]
    return pl.pallas_call(
        to_pairs_kernel,
        out_shape=[jax.ShapeDtypeStruct((modes // pairs, modes), F32)] * pairs,
        scratch_shapes=[pltpu.VMEM((modes, modes), F32)],
        compiler_params=pltpu.CompilerParams(vmem_limit_bytes=VMEM // 4),
        name="to_pairs",
    )(keep, got)


def to_modes_kernel(chips, *rest):
    parts, outs, turned = rest[: -chips - 1], rest[-chips - 1 : -1], rest[-1]
    _, span, count = outs[0].shape
    turned[...] = sum(part[...] for part in parts).T
    half = turned.shape[0] // 2
    place = lax.axis_index("mode") // 2
    for s, out in enumerate(outs):
        low = pl.multiple_of((place ^ s) * span, 8)
        out[0] = turned[pl.ds(low, span)]
        out[1] = turned[pl.ds(half + low, span)]


def to_modes(parts, chips):
    count, modes = parts[0].shape
    span = modes // 2 // chips
    return pl.pallas_call(
        functools.partial(to_modes_kernel, chips),
        out_shape=[jax.ShapeDtypeStruct((2, span, count), F32)] * chips,
        scratch_shapes=[pltpu.VMEM((modes, count), F32)],
        compiler_params=pltpu.CompilerParams(vmem_limit_bytes=VMEM // 4),
        name="to_modes",
    )(*parts)


def swap(x, axis, size, distance):
    return lax.ppermute(x, axis, [(i, i ^ distance) for i in range(size)])


def plan(modes, slices, span):
    last = 8 if span > 8 else span
    rotations, sums = [], []
    block = 0
    for tile in range(modes // LANES):
        cuts = [(0, span)]
        if tile == modes // LANES - 1 and span > last:
            cuts = [(0, span - last), (span - last, last)]
        if tile == 0 and slices > ROWS:
            rotations.append((tile, 0, ROWS, [(0, span)], ROWS // 4))
            rotations.append((tile, ROWS, slices - ROWS, cuts, ROWS))
            sums += [(tile, low, count, [(0, low), (1 + at, 0)]) for at, (low, count) in enumerate(cuts)]
            block = 1 + len(cuts)
        else:
            rotations.append((tile, 0, slices, cuts, ROWS))
            sums += [(tile, low, count, [(block + at, 0)]) for at, (low, count) in enumerate(cuts)]
            block += len(cuts)
    return rotations, sums


def shards(phi, eigvecs, freqs, occupations, smearing, probes, pair_index):
    _, slices, modes, _ = phi.shape
    pairs, parts = lax.axis_size("pair"), lax.axis_size("mode")
    span = modes // parts
    place = lax.axis_index("mode")
    others = lax.iota(jnp.int32, parts) ^ place

    def pick(table, at):
        return lax.dynamic_index_in_dim(table, pair_index[0, at], 0, keepdims=False)

    three = pick(eigvecs, 2).reshape(parts, slices, modes)[others].reshape(modes, modes).T
    rows = jnp.stack([pick(freqs, 0), pick(occupations, 0), pick(smearing, 0)])
    cols = jnp.stack([pick(freqs, 1), pick(occupations, 1), pick(smearing, 1)])
    cols = lax.dynamic_slice_in_dim(cols, place * span, span, axis=1).T
    far = list(range(parts // 2, parts))
    near = list(range(1, parts // 2))
    rotations, sums = plan(modes, slices, span)
    ready, sent, total = [], [], None

    def turn(after):
        tile, c_low, c_count, j_cuts, step = rotations.pop(0)
        tensor = phi if after is None else lax.optimization_barrier((phi, after))[0]
        ready.extend(rotate(tensor, eigvecs, pair_index, parts, tile, c_low, c_count, j_cuts, step))

    turn(None)
    for step, blocks in enumerate(ready):
        got = {0: blocks[0]}
        for s in far + near:
            block = blocks[s]
            if step > 0:
                before = [sent[-1][r] for r in (far if s == 1 else [s])]
                block, _ = lax.optimization_barrier((block, before))
            got[s] = swap(block, "mode", parts, s)
        sent.append(got)
        if rotations:
            turn(got[1])
        while sums and max(block for block, _ in sums[0][-1]) <= step:
            tile, j_low, j_count, used = sums.pop(0)
            arrived = [[sent[block][s] for block, _ in used] for s in range(parts)]
            offsets = [offset for _, offset in used]
            total = gram(arrived, offsets, three, rows, cols, probes, total, tile, j_low, j_count, 8)
    keep, give = total
    blocks = to_pairs(keep, swap(give, "mode", parts, 1), pairs)
    blocks = [b if s == 0 else swap(b, "pair", pairs, s) for s, b in enumerate(blocks)]
    blocks = to_modes(blocks, parts // 2)
    blocks = [b if s == 0 else swap(b, "mode", parts, 2 * s) for s, b in enumerate(blocks)]
    local = jnp.transpose(sum(blocks), (1, 0, 2))
    row_count, _, col_count = local.shape
    row_ids = place * row_count + jnp.arange(row_count, dtype=jnp.int32)
    col_ids = lax.axis_index("pair") * col_count + jnp.arange(col_count, dtype=jnp.int32)
    offdiag = (row_ids[:, None] != col_ids[None, :]).astype(F32)
    scale = 1.0 / (modes * math.sqrt(pairs))
    return local * offdiag[:, None, :] * scale


def shards_plain(phi, eigvecs, freqs, occupations, smearing, probes, pair_index):
    tensor = phi[0]
    slices = tensor.shape[0]
    modes = tensor.shape[1]
    q_one = pair_index[0, 0]
    q_two = pair_index[0, 1]
    q_three = pair_index[0, 2]
    e_one = lax.dynamic_index_in_dim(eigvecs, q_one, 0, keepdims=False)
    e_two = lax.dynamic_index_in_dim(eigvecs, q_two, 0, keepdims=False)
    e_three = lax.dynamic_index_in_dim(eigvecs, q_three, 0, keepdims=False)
    first = jnp.dot(
        tensor.reshape(slices * modes, modes), e_one, preferred_element_type=jnp.float32
    )
    first = first.astype(jnp.bfloat16).reshape(slices, modes, modes)
    second = jnp.einsum("cbi,bj->cji", first, e_two, preferred_element_type=jnp.float32).astype(
        jnp.bfloat16
    )
    arrived = lax.all_to_all(second, "mode", split_axis=1, concat_axis=0, tiled=True)
    span = arrived.shape[1]
    count = arrived.shape[2]
    flat = lax.dot_general(
        e_three,
        arrived.reshape(arrived.shape[0], span * count),
        (((0,), (0,)), ((), ())),
        preferred_element_type=jnp.float32,
    )
    rotated = flat.astype(jnp.bfloat16).reshape(modes, span, count)
    span = rotated.shape[1]
    offset = lax.axis_index("mode") * span
    f_two = lax.dynamic_slice_in_dim(freqs[q_two], offset, span)
    n_two = lax.dynamic_slice_in_dim(occupations[q_two], offset, span)
    h_two = lax.dynamic_slice_in_dim(smearing[q_two], offset, span)
    wgt = weights(freqs[q_one], occupations[q_one], smearing[q_one], f_two, n_two, h_two, probes[0])
    flat_rot = rotated.reshape(modes, span * modes)
    weighted = (wgt.reshape(2, 1, span * modes) * flat_rot.astype(jnp.float32)[None]).astype(
        jnp.bfloat16
    )
    pair_size = lax.axis_size("pair")
    whole = jnp.einsum("wkl,nl->kwn", weighted, flat_rot, preferred_element_type=jnp.float32)
    reduced = lax.psum_scatter(whole, "pair", scatter_dimension=2, tiled=True)
    local = lax.psum_scatter(reduced, "mode", scatter_dimension=0, tiled=True)
    row_count = local.shape[0]
    col_count = local.shape[2]
    row_ids = lax.axis_index("mode") * row_count + jnp.arange(row_count, dtype=jnp.int32)
    col_ids = lax.axis_index("pair") * col_count + jnp.arange(col_count, dtype=jnp.int32)
    offdiag = (row_ids[:, None] != col_ids[None, :]).astype(jnp.float32)
    scale = 1.0 / (modes * math.sqrt(pair_size))
    return local * offdiag[:, None, :] * scale


def solution(mesh):
    pairs, parts = mesh.shape["pair"], mesh.shape["mode"]

    def either(phi, *rest):
        _, slices, modes, _ = phi.shape
        fits = slices % ROWS == 0 and modes % LANES == 0 and slices * parts == modes
        fits = fits and parts > 3 and parts & (parts - 1) == 0 and pairs & (pairs - 1) == 0
        fits = fits and modes % (8 * pairs) == 0 and modes // parts % ROWS == 0
        return (shards if fits else shards_plain)(phi, *rest)

    return jax.shard_map(
        either,
        mesh=mesh,
        in_specs=(
            P("pair", "mode", None, None),
            P(),
            P(),
            P(),
            P(),
            P("pair", None),
            P("pair", None),
        ),
        out_specs=P("mode", None, "pair"),
        check_vma=False,
    )
```

```python
import functools
import math

import jax
import jax.numpy as jnp
from jax import lax
from jax.experimental import pallas as pl
from jax.experimental.pallas import tpu as pltpu
from jax.sharding import PartitionSpec as P

F32 = jnp.float32
BF16 = jnp.bfloat16
LANES = 128
ROWS = 16
VMEM = 60 * 2**20


def lorentz(offset, eta):
    return eta / (offset * offset + eta * eta)


def weights(f_one, n_one, h_one, f_two, n_two, h_two, omegas):
    total = f_two[:, None] + f_one[None, :]
    differ = f_two[:, None] - f_one[None, :]
    eta = 0.5 * (h_two[:, None] + h_one[None, :])
    bose_sum = 1.0 + n_one[None, :] + n_two[:, None]
    bose_diff = n_one[None, :] - n_two[:, None]
    result = []
    for probe in range(2):
        omega = omegas[probe]
        value = bose_sum * (lorentz(omega - total, eta) - lorentz(omega + total, eta))
        value = value + bose_diff * (lorentz(omega - differ, eta) - lorentz(omega + differ, eta))
        result.append(value)
    return jnp.stack(result)


def weight_pair(f_one, n_one, h_one, f_two, n_two, h_two, omega):
    total = f_two + f_one
    differ = f_two - f_one
    eta = 0.5 * (h_two + h_one)
    value = (1.0 + n_one + n_two) * (lorentz(omega - total, eta) - lorentz(omega + total, eta))
    return value + (n_one - n_two) * (lorentz(omega - differ, eta) - lorentz(omega + differ, eta))


def rotate_kernel(parts, span, j_cuts, index, phi_ref, one_ref, two_ref, *rest):
    outs, (turned_two, picked, held, turned) = rest[:-4], rest[-4:]
    j_low, j_count = j_cuts[0][0], sum(count for _, count in j_cuts)
    _, block, rows, inner = phi_ref.shape
    cols = one_ref.shape[2]
    place = lax.axis_index("mode")
    step = pl.program_id(0)

    @pl.when(step == 0)
    def _():
        turned_two[...] = two_ref[0].T
        for s in range(parts):
            low = pl.multiple_of((place ^ s) * span + j_low, ROWS)
            picked[s * j_count : (s + 1) * j_count] = turned_two[pl.ds(low, j_count)]

    first = jnp.dot(phi_ref[0].reshape(block * rows, inner), one_ref[0], preferred_element_type=F32)
    first = first.astype(BF16)
    for c in range(block):
        held[:, c * cols : (c + 1) * cols] = first[c * rows : (c + 1) * rows]
    wide = jnp.dot(picked[...], held[...], preferred_element_type=F32)
    at = lax.rem(step * block, ROWS)
    for c in range(block):
        turned[pl.ds(at + c, parts * j_count, stride=ROWS), :] = wide[:, c * cols : (c + 1) * cols]

    @pl.when(at == ROWS - block)
    def _():
        for cut, (low, count) in enumerate(j_cuts):
            for s in range(parts):
                start = (s * j_count + low - j_low) * ROWS
                piece = turned[start : start + count * ROWS].reshape(count, ROWS, cols)
                outs[cut * parts + s][...] = piece.astype(BF16)


def rotate(phi, eigvecs, pair_index, parts, tile, c_low, c_count, j_cuts, step):
    _, _, rows, inner = phi.shape
    modes = eigvecs.shape[2]
    j_count = sum(count for _, count in j_cuts)
    first_block = c_low // step
    outs = pl.pallas_call(
        functools.partial(rotate_kernel, parts, modes // parts, j_cuts),
        grid_spec=pltpu.PrefetchScalarGridSpec(
            num_scalar_prefetch=1,
            grid=(c_count // step,),
            in_specs=[
                pl.BlockSpec((1, step, rows, inner), lambda g, index: (0, first_block + g, 0, 0)),
                pl.BlockSpec((1, inner, LANES), lambda g, index: (index[0, 0], 0, tile)),
                pl.BlockSpec((1, rows, modes), lambda g, index: (index[0, 1], 0, 0)),
            ],
            out_specs=[
                pl.BlockSpec((count, ROWS, LANES), lambda g, index: (0, g * step // ROWS, 0))
                for _, count in j_cuts
                for _ in range(parts)
            ],
            scratch_shapes=[
                pltpu.VMEM((modes, rows), BF16),
                pltpu.VMEM((parts * j_count, rows), BF16),
                pltpu.VMEM((rows, step * LANES), BF16),
                pltpu.VMEM((parts * j_count * ROWS, LANES), F32),
            ],
        ),
        out_shape=[
            jax.ShapeDtypeStruct((count, c_count, LANES), BF16)
            for _, count in j_cuts
            for _ in range(parts)
        ],
        compiler_params=pltpu.CompilerParams(vmem_limit_bytes=VMEM),
        cost_estimate=pl.CostEstimate(flops=1, bytes_accessed=1, transcendentals=0),
        name="rotate",
    )(pair_index, phi, eigvecs, eigvecs)
    return [outs[cut * parts : (cut + 1) * parts] for cut in range(len(j_cuts))]


def gram_kernel(parts, c_counts, fresh, omegas, three_ref, row_ref, col_ref, *rest):
    pieces = len(c_counts)
    arrived, rest = rest[: parts * pieces], rest[parts * pieces :]
    old, (keep_ref, give_ref, side, rotated) = ((), rest) if fresh else (rest[:2], rest[2:])
    modes = three_ref.shape[0]
    slices = sum(c_counts)
    group, _, cols = arrived[0].shape
    half = modes // 2
    span = modes // parts
    core = lax.axis_index("mode") % 2

    @pl.when(pl.program_id(0) == 0)
    def _():
        for at, ref in enumerate((keep_ref, give_ref)):
            ref[...] = jnp.zeros_like(ref) if fresh else old[at][...]

    for g in range(group):
        for s in range(parts):
            low = s * slices
            for piece, count in enumerate(c_counts):
                side[low : low + count, g * cols : (g + 1) * cols] = arrived[s * pieces + piece][g]
                low += count
    rotated[...] = jnp.dot(three_ref[...], side[...], preferred_element_type=F32).astype(BF16)
    blocks = []
    for order in (core, 1 - core):
        for z in range(parts // 2):
            low = pl.multiple_of((2 * z + order) * span, ROWS)
            blocks.append(rotated[pl.ds(low, span)])
    ordered = jnp.concatenate(blocks, axis=0).astype(F32)
    scaled = []
    for w in range(2):
        weights = weight_pair(
            row_ref[0:1, :], row_ref[1:2, :], row_ref[2:3, :],
            col_ref[:, 0:1], col_ref[:, 1:2], col_ref[:, 2:3],
            omegas[0, w],
        )
        wide = jnp.concatenate([weights[g : g + 1] for g in range(group)], axis=1)
        scaled.append((ordered * wide).astype(BF16))
    sums = lax.dot_general(
        jnp.concatenate(scaled, axis=0),
        rotated[...],
        (((1,), (1,)), ((), ())),
        preferred_element_type=F32,
    )
    for w in range(2):
        keep_ref[w] += sums[2 * w * half : (2 * w + 1) * half]
        give_ref[w] += sums[(2 * w + 1) * half : (2 * w + 2) * half]


def gram(arrived, offsets, three, rows, cols, probes, old, tile, j_low, j_count, group):
    parts = len(arrived)
    pieces = [piece for one in arrived for piece in one]
    c_counts = [piece.shape[1] for piece in arrived[0]]
    blocks = [offset // group for offset in offsets] * parts
    modes = three.shape[0]
    half = modes // 2
    fresh = old is None
    whole = pl.BlockSpec((2, half, modes), lambda g: (0, 0, 0))
    return pl.pallas_call(
        functools.partial(gram_kernel, parts, c_counts, fresh),
        grid=(j_count // group,),
        in_specs=[
            pl.BlockSpec(memory_space=pltpu.SMEM),
            pl.BlockSpec((modes, modes), lambda g: (0, 0)),
            pl.BlockSpec((3, LANES), lambda g: (0, tile)),
            pl.BlockSpec((group, 3), lambda g: (j_low // group + g, 0)),
        ]
        + [
            pl.BlockSpec((group, p.shape[1], LANES), lambda g, b=b: (b + g, 0, 0))
            for p, b in zip(pieces, blocks)
        ]
        + ([] if fresh else [whole, whole]),
        out_specs=[whole, whole],
        out_shape=[jax.ShapeDtypeStruct((2, half, modes), F32)] * 2,
        scratch_shapes=[
            pltpu.VMEM((modes, group * LANES), BF16),
            pltpu.VMEM((modes, group * LANES), BF16),
        ],
        input_output_aliases={} if fresh else {4 + len(pieces): 0, 5 + len(pieces): 1},
        compiler_params=pltpu.CompilerParams(vmem_limit_bytes=VMEM // 2),
        cost_estimate=pl.CostEstimate(
            flops=int(1 * 6 * modes * modes * j_count * LANES),
            bytes_accessed=int(1 * (2 * modes * j_count * LANES + 16 * modes * modes)),
            transcendentals=0,
        ),
        name="gram",
    )(probes, three, rows, cols, *pieces, *(() if fresh else old))


def to_pairs_kernel(keep_ref, got_ref, *rest):
    outs, turned = rest[:-1], rest[-1]
    count = outs[0].shape[0]
    modes = turned.shape[0]
    turned[...] = (keep_ref[...] + got_ref[...]).reshape(modes, modes).T
    place = lax.axis_index("pair")
    for s, out in enumerate(outs):
        out[...] = turned[pl.ds(pl.multiple_of((place ^ s) * count, 8), count)]


def to_pairs(keep, got, pairs):
    modes = keep.shape[2]
    return pl.pallas_call(
        to_pairs_kernel,
        out_shape=[jax.ShapeDtypeStruct((modes // pairs, modes), F32)] * pairs,
        scratch_shapes=[pltpu.VMEM((modes, modes), F32)],
        compiler_params=pltpu.CompilerParams(vmem_limit_bytes=VMEM // 4),
        name="to_pairs",
    )(keep, got)


def to_modes_kernel(chips, *rest):
    parts, outs, turned = rest[: -chips - 1], rest[-chips - 1 : -1], rest[-1]
    _, span, count = outs[0].shape
    turned[...] = sum(part[...] for part in parts).T
    half = turned.shape[0] // 2
    place = lax.axis_index("mode") // 2
    for s, out in enumerate(outs):
        low = pl.multiple_of((place ^ s) * span, 8)
        out[0] = turned[pl.ds(low, span)]
        out[1] = turned[pl.ds(half + low, span)]


def to_modes(parts, chips):
    count, modes = parts[0].shape
    span = modes // 2 // chips
    return pl.pallas_call(
        functools.partial(to_modes_kernel, chips),
        out_shape=[jax.ShapeDtypeStruct((2, span, count), F32)] * chips,
        scratch_shapes=[pltpu.VMEM((modes, count), F32)],
        compiler_params=pltpu.CompilerParams(vmem_limit_bytes=VMEM // 4),
        name="to_modes",
    )(*parts)


def swap(x, axis, size, distance):
    return lax.ppermute(x, axis, [(i, i ^ distance) for i in range(size)])


def plan(modes, slices, span):
    last = 8 if span > 8 else span
    rotations, sums = [], []
    block = 0
    for tile in range(modes // LANES):
        cuts = [(0, span)]
        if 0 < tile < modes // LANES - 1:
            cuts = [(0, span // 2), (span // 2, span - span // 2)]
        if tile == modes // LANES - 1 and span > last:
            cuts = [(0, span - last), (span - last, last)]
        if tile == 0 and slices > ROWS:
            rotations.append((tile, 0, ROWS, [(0, span)], ROWS // 2))
            rotations.append((tile, ROWS, slices - ROWS, cuts, ROWS))
            sums += [(tile, low, count, [(0, low), (1 + at, 0)]) for at, (low, count) in enumerate(cuts)]
            block = 1 + len(cuts)
        else:
            rotations.append((tile, 0, slices, cuts, ROWS))
            sums += [(tile, low, count, [(block + at, 0)]) for at, (low, count) in enumerate(cuts)]
            block += len(cuts)
    return rotations, sums


def shards(phi, eigvecs, freqs, occupations, smearing, probes, pair_index):
    _, slices, modes, _ = phi.shape
    pairs, parts = lax.axis_size("pair"), lax.axis_size("mode")
    span = modes // parts
    place = lax.axis_index("mode")
    others = lax.iota(jnp.int32, parts) ^ place

    def pick(table, at):
        return lax.dynamic_index_in_dim(table, pair_index[0, at], 0, keepdims=False)

    three = pick(eigvecs, 2).reshape(parts, slices, modes)[others].reshape(modes, modes).T
    rows = jnp.stack([pick(freqs, 0), pick(occupations, 0), pick(smearing, 0)])
    cols = jnp.stack([pick(freqs, 1), pick(occupations, 1), pick(smearing, 1)])
    cols = lax.dynamic_slice_in_dim(cols, place * span, span, axis=1).T
    far = list(range(parts // 2, parts))[::-1]
    near = list(range(1, parts // 2))
    rotations, sums = plan(modes, slices, span)
    ready, sent, total = [], [], None

    def turn(after):
        tile, c_low, c_count, j_cuts, step = rotations.pop(0)
        tensor = phi if after is None else lax.optimization_barrier((phi, after))[0]
        ready.extend(rotate(tensor, eigvecs, pair_index, parts, tile, c_low, c_count, j_cuts, step))

    turn(None)
    for step, blocks in enumerate(ready):
        got = {0: blocks[0]}
        for s in far + near:
            block = blocks[s]
            if step > 0:
                before = [sent[-1][r] for r in (far if s == 1 else [s])]
                block, _ = lax.optimization_barrier((block, before))
            got[s] = swap(block, "mode", parts, s)
        sent.append(got)
        if rotations:
            turn(got[1])
        while sums and max(block for block, _ in sums[0][-1]) <= step:
            tile, j_low, j_count, used = sums.pop(0)
            arrived = [[sent[block][s] for block, _ in used] for s in range(parts)]
            offsets = [offset for _, offset in used]
            total = gram(arrived, offsets, three, rows, cols, probes, total, tile, j_low, j_count, 8)
    keep, give = total
    blocks = to_pairs(keep, swap(give, "mode", parts, 1), pairs)
    blocks = [b if s == 0 else swap(b, "pair", pairs, s) for s, b in enumerate(blocks)]
    blocks = to_modes(blocks, parts // 2)
    blocks = [b if s == 0 else swap(b, "mode", parts, 2 * s) for s, b in enumerate(blocks)]
    local = jnp.transpose(sum(blocks), (1, 0, 2))
    row_count, _, col_count = local.shape
    row_ids = place * row_count + jnp.arange(row_count, dtype=jnp.int32)
    col_ids = lax.axis_index("pair") * col_count + jnp.arange(col_count, dtype=jnp.int32)
    offdiag = (row_ids[:, None] != col_ids[None, :]).astype(F32)
    scale = 1.0 / (modes * math.sqrt(pairs))
    return local * offdiag[:, None, :] * scale


def shards_plain(phi, eigvecs, freqs, occupations, smearing, probes, pair_index):
    tensor = phi[0]
    slices = tensor.shape[0]
    modes = tensor.shape[1]
    q_one = pair_index[0, 0]
    q_two = pair_index[0, 1]
    q_three = pair_index[0, 2]
    e_one = lax.dynamic_index_in_dim(eigvecs, q_one, 0, keepdims=False)
    e_two = lax.dynamic_index_in_dim(eigvecs, q_two, 0, keepdims=False)
    e_three = lax.dynamic_index_in_dim(eigvecs, q_three, 0, keepdims=False)
    first = jnp.dot(
        tensor.reshape(slices * modes, modes), e_one, preferred_element_type=jnp.float32
    )
    first = first.astype(jnp.bfloat16).reshape(slices, modes, modes)
    second = jnp.einsum("cbi,bj->cji", first, e_two, preferred_element_type=jnp.float32).astype(
        jnp.bfloat16
    )
    arrived = lax.all_to_all(second, "mode", split_axis=1, concat_axis=0, tiled=True)
    span = arrived.shape[1]
    count = arrived.shape[2]
    flat = lax.dot_general(
        e_three,
        arrived.reshape(arrived.shape[0], span * count),
        (((0,), (0,)), ((), ())),
        preferred_element_type=jnp.float32,
    )
    rotated = flat.astype(jnp.bfloat16).reshape(modes, span, count)
    span = rotated.shape[1]
    offset = lax.axis_index("mode") * span
    f_two = lax.dynamic_slice_in_dim(freqs[q_two], offset, span)
    n_two = lax.dynamic_slice_in_dim(occupations[q_two], offset, span)
    h_two = lax.dynamic_slice_in_dim(smearing[q_two], offset, span)
    wgt = weights(freqs[q_one], occupations[q_one], smearing[q_one], f_two, n_two, h_two, probes[0])
    flat_rot = rotated.reshape(modes, span * modes)
    weighted = (wgt.reshape(2, 1, span * modes) * flat_rot.astype(jnp.float32)[None]).astype(
        jnp.bfloat16
    )
    pair_size = lax.axis_size("pair")
    whole = jnp.einsum("wkl,nl->kwn", weighted, flat_rot, preferred_element_type=jnp.float32)
    reduced = lax.psum_scatter(whole, "pair", scatter_dimension=2, tiled=True)
    local = lax.psum_scatter(reduced, "mode", scatter_dimension=0, tiled=True)
    row_count = local.shape[0]
    col_count = local.shape[2]
    row_ids = lax.axis_index("mode") * row_count + jnp.arange(row_count, dtype=jnp.int32)
    col_ids = lax.axis_index("pair") * col_count + jnp.arange(col_count, dtype=jnp.int32)
    offdiag = (row_ids[:, None] != col_ids[None, :]).astype(jnp.float32)
    scale = 1.0 / (modes * math.sqrt(pair_size))
    return local * offdiag[:, None, :] * scale


def solution(mesh):
    pairs, parts = mesh.shape["pair"], mesh.shape["mode"]

    def either(phi, *rest):
        _, slices, modes, _ = phi.shape
        fits = slices % ROWS == 0 and modes % LANES == 0 and slices * parts == modes
        fits = fits and parts > 3 and parts & (parts - 1) == 0 and pairs & (pairs - 1) == 0
        fits = fits and modes % (8 * pairs) == 0 and modes // parts % ROWS == 0
        return (shards if fits else shards_plain)(phi, *rest)

    return jax.shard_map(
        either,
        mesh=mesh,
        in_specs=(
            P("pair", "mode", None, None),
            P(),
            P(),
            P(),
            P(),
            P("pair", None),
            P("pair", None),
        ),
        out_specs=P("mode", None, "pair"),
        check_vma=False,
    )
```

```python
import functools
import math

import jax
import jax.numpy as jnp
from jax import lax
from jax.experimental import pallas as pl
from jax.experimental.pallas import tpu as pltpu
from jax.sharding import PartitionSpec as P

F32 = jnp.float32
BF16 = jnp.bfloat16
LANES = 128
ROWS = 16
VMEM = 60 * 2**20


def lorentz(offset, eta):
    return eta / (offset * offset + eta * eta)


def weights(f_one, n_one, h_one, f_two, n_two, h_two, omegas):
    total = f_two[:, None] + f_one[None, :]
    differ = f_two[:, None] - f_one[None, :]
    eta = 0.5 * (h_two[:, None] + h_one[None, :])
    bose_sum = 1.0 + n_one[None, :] + n_two[:, None]
    bose_diff = n_one[None, :] - n_two[:, None]
    result = []
    for probe in range(2):
        omega = omegas[probe]
        value = bose_sum * (lorentz(omega - total, eta) - lorentz(omega + total, eta))
        value = value + bose_diff * (lorentz(omega - differ, eta) - lorentz(omega + differ, eta))
        result.append(value)
    return jnp.stack(result)


def weight_pair(f_one, n_one, h_one, f_two, n_two, h_two, omega):
    total = f_two + f_one
    differ = f_two - f_one
    eta = 0.5 * (h_two + h_one)
    value = (1.0 + n_one + n_two) * (lorentz(omega - total, eta) - lorentz(omega + total, eta))
    return value + (n_one - n_two) * (lorentz(omega - differ, eta) - lorentz(omega + differ, eta))


def rotate_kernel(parts, span, j_cuts, index, phi_ref, one_ref, two_ref, *rest):
    outs, (turned_two, picked, held, turned) = rest[:-4], rest[-4:]
    j_low, j_count = j_cuts[0][0], sum(count for _, count in j_cuts)
    _, block, rows, inner = phi_ref.shape
    cols = one_ref.shape[2]
    place = lax.axis_index("mode")
    step = pl.program_id(0)

    @pl.when(step == 0)
    def _():
        turned_two[...] = two_ref[0].T
        for s in range(parts):
            low = pl.multiple_of((place ^ s) * span + j_low, ROWS)
            picked[s * j_count : (s + 1) * j_count] = turned_two[pl.ds(low, j_count)]

    first = jnp.dot(phi_ref[0].reshape(block * rows, inner), one_ref[0], preferred_element_type=F32)
    first = first.astype(BF16)
    for c in range(block):
        held[:, c * cols : (c + 1) * cols] = first[c * rows : (c + 1) * rows]
    wide = jnp.dot(picked[...], held[...], preferred_element_type=F32)
    at = lax.rem(step * block, ROWS)
    for c in range(block):
        turned[pl.ds(at + c, parts * j_count, stride=ROWS), :] = wide[:, c * cols : (c + 1) * cols]

    @pl.when(at == ROWS - block)
    def _():
        for cut, (low, count) in enumerate(j_cuts):
            for s in range(parts):
                start = (s * j_count + low - j_low) * ROWS
                piece = turned[start : start + count * ROWS].reshape(count, ROWS, cols)
                outs[cut * parts + s][...] = piece.astype(BF16)


def rotate(phi, eigvecs, pair_index, parts, tile, c_low, c_count, j_cuts, step):
    _, _, rows, inner = phi.shape
    modes = eigvecs.shape[2]
    j_count = sum(count for _, count in j_cuts)
    first_block = c_low // step
    outs = pl.pallas_call(
        functools.partial(rotate_kernel, parts, modes // parts, j_cuts),
        grid_spec=pltpu.PrefetchScalarGridSpec(
            num_scalar_prefetch=1,
            grid=(c_count // step,),
            in_specs=[
                pl.BlockSpec((1, step, rows, inner), lambda g, index: (0, first_block + g, 0, 0)),
                pl.BlockSpec((1, inner, LANES), lambda g, index: (index[0, 0], 0, tile)),
                pl.BlockSpec((1, rows, modes), lambda g, index: (index[0, 1], 0, 0)),
            ],
            out_specs=[
                pl.BlockSpec((count, ROWS, LANES), lambda g, index: (0, g * step // ROWS, 0))
                for _, count in j_cuts
                for _ in range(parts)
            ],
            scratch_shapes=[
                pltpu.VMEM((modes, rows), BF16),
                pltpu.VMEM((parts * j_count, rows), BF16),
                pltpu.VMEM((rows, step * LANES), BF16),
                pltpu.VMEM((parts * j_count * ROWS + ROWS, LANES), F32),
            ],
        ),
        out_shape=[
            jax.ShapeDtypeStruct((count, c_count, LANES), BF16)
            for _, count in j_cuts
            for _ in range(parts)
        ],
        compiler_params=pltpu.CompilerParams(vmem_limit_bytes=VMEM),
        cost_estimate=pl.CostEstimate(flops=1, bytes_accessed=1, transcendentals=0),
        name="rotate",
    )(pair_index, phi, eigvecs, eigvecs)
    return [outs[cut * parts : (cut + 1) * parts] for cut in range(len(j_cuts))]


def gram_kernel(parts, c_counts, fresh, omegas, three_ref, row_ref, col_ref, *rest):
    pieces = len(c_counts)
    arrived, rest = rest[: parts * pieces], rest[parts * pieces :]
    old, (keep_ref, give_ref, side, rotated) = ((), rest) if fresh else (rest[:2], rest[2:])
    modes = three_ref.shape[0]
    slices = sum(c_counts)
    group, _, cols = arrived[0].shape
    half = modes // 2
    span = modes // parts
    core = lax.axis_index("mode") % 2

    @pl.when(pl.program_id(0) == 0)
    def _():
        for at, ref in enumerate((keep_ref, give_ref)):
            ref[...] = jnp.zeros_like(ref) if fresh else old[at][...]

    for g in range(group):
        for s in range(parts):
            low = s * slices
            for piece, count in enumerate(c_counts):
                side[low : low + count, g * cols : (g + 1) * cols] = arrived[s * pieces + piece][g]
                low += count
    rotated[...] = jnp.dot(three_ref[...], side[...], preferred_element_type=F32).astype(BF16)
    blocks = []
    for order in (core, 1 - core):
        for z in range(parts // 2):
            low = pl.multiple_of((2 * z + order) * span, ROWS)
            blocks.append(rotated[pl.ds(low, span)])
    ordered = jnp.concatenate(blocks, axis=0).astype(F32)
    scaled = []
    for w in range(2):
        weights = weight_pair(
            row_ref[0:1, :], row_ref[1:2, :], row_ref[2:3, :],
            col_ref[:, 0:1], col_ref[:, 1:2], col_ref[:, 2:3],
            omegas[0, w],
        )
        wide = jnp.concatenate([weights[g : g + 1] for g in range(group)], axis=1)
        scaled.append((ordered * wide).astype(BF16))
    sums = lax.dot_general(
        jnp.concatenate(scaled, axis=0),
        rotated[...],
        (((1,), (1,)), ((), ())),
        preferred_element_type=F32,
    )
    for w in range(2):
        keep_ref[w] += sums[2 * w * half : (2 * w + 1) * half]
        give_ref[w] += sums[(2 * w + 1) * half : (2 * w + 2) * half]


def gram(arrived, offsets, three, rows, cols, probes, old, tile, j_low, j_count, group):
    parts = len(arrived)
    pieces = [piece for one in arrived for piece in one]
    c_counts = [piece.shape[1] for piece in arrived[0]]
    blocks = [offset // group for offset in offsets] * parts
    modes = three.shape[0]
    half = modes // 2
    fresh = old is None
    whole = pl.BlockSpec((2, half, modes), lambda g: (0, 0, 0))
    return pl.pallas_call(
        functools.partial(gram_kernel, parts, c_counts, fresh),
        grid=(j_count // group,),
        in_specs=[
            pl.BlockSpec(memory_space=pltpu.SMEM),
            pl.BlockSpec((modes, modes), lambda g: (0, 0)),
            pl.BlockSpec((3, LANES), lambda g: (0, tile)),
            pl.BlockSpec((group, 3), lambda g: (j_low // group + g, 0)),
        ]
        + [
            pl.BlockSpec((group, p.shape[1], LANES), lambda g, b=b: (b + g, 0, 0))
            for p, b in zip(pieces, blocks)
        ]
        + ([] if fresh else [whole, whole]),
        out_specs=[whole, whole],
        out_shape=[jax.ShapeDtypeStruct((2, half, modes), F32)] * 2,
        scratch_shapes=[
            pltpu.VMEM((modes, group * LANES), BF16),
            pltpu.VMEM((modes, group * LANES), BF16),
        ],
        input_output_aliases={} if fresh else {4 + len(pieces): 0, 5 + len(pieces): 1},
        compiler_params=pltpu.CompilerParams(vmem_limit_bytes=VMEM // 2),
        cost_estimate=pl.CostEstimate(
            flops=6 * modes * modes * j_count * LANES,
            bytes_accessed=2 * modes * j_count * LANES + 16 * modes * modes,
            transcendentals=0,
        ),
        name="gram",
    )(probes, three, rows, cols, *pieces, *(() if fresh else old))


def to_pairs_kernel(keep_ref, got_ref, *rest):
    outs, turned = rest[:-1], rest[-1]
    count = outs[0].shape[0]
    modes = turned.shape[0]
    turned[...] = (keep_ref[...] + got_ref[...]).reshape(modes, modes).T
    place = lax.axis_index("pair")
    for s, out in enumerate(outs):
        out[...] = turned[pl.ds(pl.multiple_of((place ^ s) * count, 8), count)]


def to_pairs(keep, got, pairs):
    modes = keep.shape[2]
    return pl.pallas_call(
        to_pairs_kernel,
        out_shape=[jax.ShapeDtypeStruct((modes // pairs, modes), F32)] * pairs,
        scratch_shapes=[pltpu.VMEM((modes, modes), F32)],
        compiler_params=pltpu.CompilerParams(vmem_limit_bytes=VMEM // 4),
        name="to_pairs",
    )(keep, got)


def to_modes_kernel(chips, *rest):
    parts, outs, turned = rest[: -chips - 1], rest[-chips - 1 : -1], rest[-1]
    _, span, count = outs[0].shape
    turned[...] = sum(part[...] for part in parts).T
    half = turned.shape[0] // 2
    place = lax.axis_index("mode") // 2
    for s, out in enumerate(outs):
        low = pl.multiple_of((place ^ s) * span, 8)
        out[0] = turned[pl.ds(low, span)]
        out[1] = turned[pl.ds(half + low, span)]


def to_modes(parts, chips):
    count, modes = parts[0].shape
    span = modes // 2 // chips
    return pl.pallas_call(
        functools.partial(to_modes_kernel, chips),
        out_shape=[jax.ShapeDtypeStruct((2, span, count), F32)] * chips,
        scratch_shapes=[pltpu.VMEM((modes, count), F32)],
        compiler_params=pltpu.CompilerParams(vmem_limit_bytes=VMEM // 4),
        name="to_modes",
    )(*parts)


def swap(x, axis, size, distance):
    return lax.ppermute(x, axis, [(i, i ^ distance) for i in range(size)])


def plan(modes, slices, span):
    last = 8 if span > 8 else span
    rotations, sums = [], []
    block = 0
    for tile in range(modes // LANES):
        cuts = [(0, span)]
        if 0 < tile < modes // LANES - 1:
            cuts = [(0, span // 2), (span // 2, span - span // 2)]
        if tile == modes // LANES - 1 and span > last:
            cuts = [(0, span - last), (span - last, last)]
        if tile == 0 and slices > ROWS:
            rotations.append((tile, 0, ROWS, [(0, span)], ROWS // 2))
            rotations.append((tile, ROWS, slices - ROWS, cuts, ROWS))
            sums += [(tile, low, count, [(0, low), (1 + at, 0)]) for at, (low, count) in enumerate(cuts)]
            block = 1 + len(cuts)
        else:
            rotations.append((tile, 0, slices, cuts, ROWS))
            sums += [(tile, low, count, [(block + at, 0)]) for at, (low, count) in enumerate(cuts)]
            block += len(cuts)
    return rotations, sums


def shards(phi, eigvecs, freqs, occupations, smearing, probes, pair_index):
    _, slices, modes, _ = phi.shape
    pairs, parts = lax.axis_size("pair"), lax.axis_size("mode")
    span = modes // parts
    place = lax.axis_index("mode")
    others = lax.iota(jnp.int32, parts) ^ place

    def pick(table, at):
        return lax.dynamic_index_in_dim(table, pair_index[0, at], 0, keepdims=False)

    three = pick(eigvecs, 2).reshape(parts, slices, modes)[others].reshape(modes, modes).T
    rows = jnp.stack([pick(freqs, 0), pick(occupations, 0), pick(smearing, 0)])
    cols = jnp.stack([pick(freqs, 1), pick(occupations, 1), pick(smearing, 1)])
    cols = lax.dynamic_slice_in_dim(cols, place * span, span, axis=1).T
    far = list(range(parts // 2, parts))[::-1]
    near = list(range(1, parts // 2))
    rotations, sums = plan(modes, slices, span)
    ready, sent, total = [], [], None

    def turn(after):
        tile, c_low, c_count, j_cuts, step = rotations.pop(0)
        tensor = phi if after is None else lax.optimization_barrier((phi, after))[0]
        ready.extend(rotate(tensor, eigvecs, pair_index, parts, tile, c_low, c_count, j_cuts, step))

    turn(None)
    for step, blocks in enumerate(ready):
        got = {0: blocks[0]}
        for s in far + near:
            block = blocks[s]
            if step > 0:
                before = [sent[-1][r] for r in (far if s == 1 else [s])]
                block, _ = lax.optimization_barrier((block, before))
            got[s] = swap(block, "mode", parts, s)
        sent.append(got)
        if rotations:
            turn(got[1])
        while sums and max(block for block, _ in sums[0][-1]) <= step:
            tile, j_low, j_count, used = sums.pop(0)
            arrived = [[sent[block][s] for block, _ in used] for s in range(parts)]
            offsets = [offset for _, offset in used]
            total = gram(arrived, offsets, three, rows, cols, probes, total, tile, j_low, j_count, 8)
    keep, give = total
    blocks = to_pairs(keep, swap(give, "mode", parts, 1), pairs)
    blocks = [b if s == 0 else swap(b, "pair", pairs, s) for s, b in enumerate(blocks)]
    blocks = to_modes(blocks, parts // 2)
    blocks = [b if s == 0 else swap(b, "mode", parts, 2 * s) for s, b in enumerate(blocks)]
    local = jnp.transpose(sum(blocks), (1, 0, 2))
    row_count, _, col_count = local.shape
    row_ids = place * row_count + jnp.arange(row_count, dtype=jnp.int32)
    col_ids = lax.axis_index("pair") * col_count + jnp.arange(col_count, dtype=jnp.int32)
    offdiag = (row_ids[:, None] != col_ids[None, :]).astype(F32)
    scale = 1.0 / (modes * math.sqrt(pairs))
    return local * offdiag[:, None, :] * scale


def shards_plain(phi, eigvecs, freqs, occupations, smearing, probes, pair_index):
    tensor = phi[0]
    slices = tensor.shape[0]
    modes = tensor.shape[1]
    q_one = pair_index[0, 0]
    q_two = pair_index[0, 1]
    q_three = pair_index[0, 2]
    e_one = lax.dynamic_index_in_dim(eigvecs, q_one, 0, keepdims=False)
    e_two = lax.dynamic_index_in_dim(eigvecs, q_two, 0, keepdims=False)
    e_three = lax.dynamic_index_in_dim(eigvecs, q_three, 0, keepdims=False)
    first = jnp.dot(
        tensor.reshape(slices * modes, modes), e_one, preferred_element_type=jnp.float32
    )
    first = first.astype(jnp.bfloat16).reshape(slices, modes, modes)
    second = jnp.einsum("cbi,bj->cji", first, e_two, preferred_element_type=jnp.float32).astype(
        jnp.bfloat16
    )
    arrived = lax.all_to_all(second, "mode", split_axis=1, concat_axis=0, tiled=True)
    span = arrived.shape[1]
    count = arrived.shape[2]
    flat = lax.dot_general(
        e_three,
        arrived.reshape(arrived.shape[0], span * count),
        (((0,), (0,)), ((), ())),
        preferred_element_type=jnp.float32,
    )
    rotated = flat.astype(jnp.bfloat16).reshape(modes, span, count)
    span = rotated.shape[1]
    offset = lax.axis_index("mode") * span
    f_two = lax.dynamic_slice_in_dim(freqs[q_two], offset, span)
    n_two = lax.dynamic_slice_in_dim(occupations[q_two], offset, span)
    h_two = lax.dynamic_slice_in_dim(smearing[q_two], offset, span)
    wgt = weights(freqs[q_one], occupations[q_one], smearing[q_one], f_two, n_two, h_two, probes[0])
    flat_rot = rotated.reshape(modes, span * modes)
    weighted = (wgt.reshape(2, 1, span * modes) * flat_rot.astype(jnp.float32)[None]).astype(
        jnp.bfloat16
    )
    pair_size = lax.axis_size("pair")
    whole = jnp.einsum("wkl,nl->kwn", weighted, flat_rot, preferred_element_type=jnp.float32)
    reduced = lax.psum_scatter(whole, "pair", scatter_dimension=2, tiled=True)
    local = lax.psum_scatter(reduced, "mode", scatter_dimension=0, tiled=True)
    row_count = local.shape[0]
    col_count = local.shape[2]
    row_ids = lax.axis_index("mode") * row_count + jnp.arange(row_count, dtype=jnp.int32)
    col_ids = lax.axis_index("pair") * col_count + jnp.arange(col_count, dtype=jnp.int32)
    offdiag = (row_ids[:, None] != col_ids[None, :]).astype(jnp.float32)
    scale = 1.0 / (modes * math.sqrt(pair_size))
    return local * offdiag[:, None, :] * scale


def solution(mesh):
    pairs, parts = mesh.shape["pair"], mesh.shape["mode"]

    def either(phi, *rest):
        _, slices, modes, _ = phi.shape
        fits = slices % ROWS == 0 and modes % LANES == 0 and slices * parts == modes
        fits = fits and parts > 3 and parts & (parts - 1) == 0 and pairs & (pairs - 1) == 0
        fits = fits and modes % (8 * pairs) == 0 and modes // parts % ROWS == 0
        return (shards if fits else shards_plain)(phi, *rest)

    return jax.shard_map(
        either,
        mesh=mesh,
        in_specs=(
            P("pair", "mode", None, None),
            P(),
            P(),
            P(),
            P(),
            P("pair", None),
            P("pair", None),
        ),
        out_specs=P("mode", None, "pair"),
        check_vma=False,
    )
```

```python
import functools
import math

import jax
import jax.numpy as jnp
from jax import lax
from jax.experimental import pallas as pl
from jax.experimental.pallas import tpu as pltpu
from jax.sharding import PartitionSpec as P

F32 = jnp.float32
BF16 = jnp.bfloat16
LANES = 128
ROWS = 16
VMEM = 60 * 2**20


def lorentz(offset, eta):
    return eta / (offset * offset + eta * eta)


def weights(f_one, n_one, h_one, f_two, n_two, h_two, omegas):
    total = f_two[:, None] + f_one[None, :]
    differ = f_two[:, None] - f_one[None, :]
    eta = 0.5 * (h_two[:, None] + h_one[None, :])
    bose_sum = 1.0 + n_one[None, :] + n_two[:, None]
    bose_diff = n_one[None, :] - n_two[:, None]
    result = []
    for probe in range(2):
        omega = omegas[probe]
        value = bose_sum * (lorentz(omega - total, eta) - lorentz(omega + total, eta))
        value = value + bose_diff * (lorentz(omega - differ, eta) - lorentz(omega + differ, eta))
        result.append(value)
    return jnp.stack(result)


def weight_pair(f_one, n_one, h_one, f_two, n_two, h_two, omega):
    total = f_two + f_one
    differ = f_two - f_one
    eta = 0.5 * (h_two + h_one)
    value = (1.0 + n_one + n_two) * (lorentz(omega - total, eta) - lorentz(omega + total, eta))
    return value + (n_one - n_two) * (lorentz(omega - differ, eta) - lorentz(omega + differ, eta))


def rotate_kernel(parts, span, j_cuts, index, phi_ref, one_ref, two_ref, *rest):
    outs, (turned_two, picked, held, turned) = rest[:-4], rest[-4:]
    j_low, j_count = j_cuts[0][0], sum(count for _, count in j_cuts)
    _, block, rows, inner = phi_ref.shape
    cols = one_ref.shape[2]
    place = lax.axis_index("mode")
    step = pl.program_id(0)

    @pl.when(step == 0)
    def _():
        turned_two[...] = two_ref[0].T
        for s in range(parts):
            low = pl.multiple_of((place ^ s) * span + j_low, ROWS)
            picked[s * j_count : (s + 1) * j_count] = turned_two[pl.ds(low, j_count)]

    first = jnp.dot(phi_ref[0].reshape(block * rows, inner), one_ref[0], preferred_element_type=F32)
    first = first.astype(BF16)
    for c in range(block):
        held[:, c * cols : (c + 1) * cols] = first[c * rows : (c + 1) * rows]
    wide = jnp.dot(picked[...], held[...], preferred_element_type=F32)
    at = lax.rem(step * block, ROWS)
    for c in range(block):
        turned[pl.ds(at + c, parts * j_count, stride=ROWS), :] = wide[:, c * cols : (c + 1) * cols]

    @pl.when(at == ROWS - block)
    def _():
        for cut, (low, count) in enumerate(j_cuts):
            for s in range(parts):
                start = (s * j_count + low - j_low) * ROWS
                piece = turned[start : start + count * ROWS].reshape(count, ROWS, cols)
                outs[cut * parts + s][...] = piece.astype(BF16)


def rotate(phi, eigvecs, pair_index, parts, tile, c_low, c_count, j_cuts, step):
    _, _, rows, inner = phi.shape
    modes = eigvecs.shape[2]
    j_count = sum(count for _, count in j_cuts)
    first_block = c_low // step
    outs = pl.pallas_call(
        functools.partial(rotate_kernel, parts, modes // parts, j_cuts),
        grid_spec=pltpu.PrefetchScalarGridSpec(
            num_scalar_prefetch=1,
            grid=(c_count // step,),
            in_specs=[
                pl.BlockSpec((1, step, rows, inner), lambda g, index: (0, first_block + g, 0, 0)),
                pl.BlockSpec((1, inner, LANES), lambda g, index: (index[0, 0], 0, tile)),
                pl.BlockSpec((1, rows, modes), lambda g, index: (index[0, 1], 0, 0)),
            ],
            out_specs=[
                pl.BlockSpec((count, ROWS, LANES), lambda g, index: (0, g * step // ROWS, 0))
                for _, count in j_cuts
                for _ in range(parts)
            ],
            scratch_shapes=[
                pltpu.VMEM((modes, rows), BF16),
                pltpu.VMEM((parts * j_count, rows), BF16),
                pltpu.VMEM((rows, step * LANES), BF16),
                pltpu.VMEM((parts * j_count * ROWS + ROWS, LANES), F32),
            ],
        ),
        out_shape=[
            jax.ShapeDtypeStruct((count, c_count, LANES), BF16)
            for _, count in j_cuts
            for _ in range(parts)
        ],
        compiler_params=pltpu.CompilerParams(vmem_limit_bytes=VMEM),
        cost_estimate=pl.CostEstimate(flops=1, bytes_accessed=1, transcendentals=0),
        name="rotate",
    )(pair_index, phi, eigvecs, eigvecs)
    return [outs[cut * parts : (cut + 1) * parts] for cut in range(len(j_cuts))]


def gram_kernel(parts, c_counts, fresh, omegas, three_ref, row_ref, col_ref, *rest):
    pieces = len(c_counts)
    arrived, rest = rest[: parts * pieces], rest[parts * pieces :]
    old, (keep_ref, give_ref, side, rotated) = ((), rest) if fresh else (rest[:2], rest[2:])
    modes = three_ref.shape[0]
    slices = sum(c_counts)
    group, _, cols = arrived[0].shape
    half = modes // 2
    span = modes // parts
    core = lax.axis_index("mode") % 2

    @pl.when(pl.program_id(0) == 0)
    def _():
        for at, ref in enumerate((keep_ref, give_ref)):
            ref[...] = jnp.zeros_like(ref) if fresh else old[at][...]

    for g in range(group):
        for s in range(parts):
            low = s * slices
            for piece, count in enumerate(c_counts):
                side[low : low + count, g * cols : (g + 1) * cols] = arrived[s * pieces + piece][g]
                low += count
    rotated[...] = jnp.dot(three_ref[...], side[...], preferred_element_type=F32).astype(BF16)
    blocks = []
    for order in (core, 1 - core):
        for z in range(parts // 2):
            low = pl.multiple_of((2 * z + order) * span, ROWS)
            blocks.append(rotated[pl.ds(low, span)])
    ordered = jnp.concatenate(blocks, axis=0).astype(F32)
    scaled = []
    for w in range(2):
        weights = weight_pair(
            row_ref[0:1, :], row_ref[1:2, :], row_ref[2:3, :],
            col_ref[:, 0:1], col_ref[:, 1:2], col_ref[:, 2:3],
            omegas[0, w],
        )
        wide = jnp.concatenate([weights[g : g + 1] for g in range(group)], axis=1)
        scaled.append((ordered * wide).astype(BF16))
    sums = lax.dot_general(
        jnp.concatenate(scaled, axis=0),
        rotated[...],
        (((1,), (1,)), ((), ())),
        preferred_element_type=F32,
    )
    for w in range(2):
        keep_ref[w] += sums[2 * w * half : (2 * w + 1) * half]
        give_ref[w] += sums[(2 * w + 1) * half : (2 * w + 2) * half]


def gram(arrived, offsets, three, rows, cols, probes, old, tile, j_low, j_count, group):
    parts = len(arrived)
    pieces = [piece for one in arrived for piece in one]
    c_counts = [piece.shape[1] for piece in arrived[0]]
    blocks = [offset // group for offset in offsets] * parts
    modes = three.shape[0]
    half = modes // 2
    fresh = old is None
    whole = pl.BlockSpec((2, half, modes), lambda g: (0, 0, 0))
    return pl.pallas_call(
        functools.partial(gram_kernel, parts, c_counts, fresh),
        grid=(j_count // group,),
        in_specs=[
            pl.BlockSpec(memory_space=pltpu.SMEM),
            pl.BlockSpec((modes, modes), lambda g: (0, 0)),
            pl.BlockSpec((3, LANES), lambda g: (0, tile)),
            pl.BlockSpec((group, 3), lambda g: (j_low // group + g, 0)),
        ]
        + [
            pl.BlockSpec((group, p.shape[1], LANES), lambda g, b=b: (b + g, 0, 0))
            for p, b in zip(pieces, blocks)
        ]
        + ([] if fresh else [whole, whole]),
        out_specs=[whole, whole],
        out_shape=[jax.ShapeDtypeStruct((2, half, modes), F32)] * 2,
        scratch_shapes=[
            pltpu.VMEM((modes, group * LANES), BF16),
            pltpu.VMEM((modes, group * LANES), BF16),
        ],
        input_output_aliases={} if fresh else {4 + len(pieces): 0, 5 + len(pieces): 1},
        compiler_params=pltpu.CompilerParams(vmem_limit_bytes=VMEM // 2),
        cost_estimate=pl.CostEstimate(
            flops=6 * modes * modes * j_count * LANES,
            bytes_accessed=2 * modes * j_count * LANES + 16 * modes * modes,
            transcendentals=0,
        ),
        name="gram",
    )(probes, three, rows, cols, *pieces, *(() if fresh else old))


def to_pairs_kernel(keep_ref, got_ref, *rest):
    outs, turned = rest[:-1], rest[-1]
    count = outs[0].shape[0]
    modes = turned.shape[0]
    turned[...] = (keep_ref[...] + got_ref[...]).reshape(modes, modes).T
    place = lax.axis_index("pair")
    for s, out in enumerate(outs):
        out[...] = turned[pl.ds(pl.multiple_of((place ^ s) * count, 8), count)]


def to_pairs(keep, got, pairs):
    modes = keep.shape[2]
    return pl.pallas_call(
        to_pairs_kernel,
        out_shape=[jax.ShapeDtypeStruct((modes // pairs, modes), F32)] * pairs,
        scratch_shapes=[pltpu.VMEM((modes, modes), F32)],
        compiler_params=pltpu.CompilerParams(vmem_limit_bytes=VMEM // 4),
        name="to_pairs",
    )(keep, got)


def to_modes_kernel(chips, *rest):
    parts, outs, turned = rest[: -chips - 1], rest[-chips - 1 : -1], rest[-1]
    _, span, count = outs[0].shape
    turned[...] = sum(part[...] for part in parts).T
    half = turned.shape[0] // 2
    place = lax.axis_index("mode") // 2
    for s, out in enumerate(outs):
        low = pl.multiple_of((place ^ s) * span, 8)
        out[0] = turned[pl.ds(low, span)]
        out[1] = turned[pl.ds(half + low, span)]


def to_modes(parts, chips):
    count, modes = parts[0].shape
    span = modes // 2 // chips
    return pl.pallas_call(
        functools.partial(to_modes_kernel, chips),
        out_shape=[jax.ShapeDtypeStruct((2, span, count), F32)] * chips,
        scratch_shapes=[pltpu.VMEM((modes, count), F32)],
        compiler_params=pltpu.CompilerParams(vmem_limit_bytes=VMEM // 4),
        name="to_modes",
    )(*parts)


def swap(x, axis, size, distance):
    return lax.ppermute(x, axis, [(i, i ^ distance) for i in range(size)])


def plan(modes, slices, span):
    last = 8 if span > 8 else span
    rotations, sums = [], []
    block = 0
    for tile in range(modes // LANES):
        cuts = [(0, span)]
        if 0 < tile < modes // LANES - 1:
            cuts = [(0, span // 2), (span // 2, span - span // 2)]
        if tile == modes // LANES - 1 and span > last:
            cuts = [(0, span - last), (span - last, last)]
        if tile == 0 and slices > ROWS:
            rotations.append((tile, 0, ROWS, [(0, span)], ROWS // 2))
            rotations.append((tile, ROWS, slices - ROWS, cuts, ROWS))
            sums += [(tile, low, count, [(0, low), (1 + at, 0)]) for at, (low, count) in enumerate(cuts)]
            block = 1 + len(cuts)
        else:
            rotations.append((tile, 0, slices, cuts, ROWS))
            sums += [(tile, low, count, [(block + at, 0)]) for at, (low, count) in enumerate(cuts)]
            block += len(cuts)
    return rotations, sums


def shards(phi, eigvecs, freqs, occupations, smearing, probes, pair_index):
    _, slices, modes, _ = phi.shape
    pairs, parts = lax.axis_size("pair"), lax.axis_size("mode")
    span = modes // parts
    place = lax.axis_index("mode")
    others = lax.iota(jnp.int32, parts) ^ place

    def pick(table, at):
        return lax.dynamic_index_in_dim(table, pair_index[0, at], 0, keepdims=False)

    three = pick(eigvecs, 2).reshape(parts, slices, modes)[others].reshape(modes, modes).T
    rows = jnp.stack([pick(freqs, 0), pick(occupations, 0), pick(smearing, 0)])
    cols = jnp.stack([pick(freqs, 1), pick(occupations, 1), pick(smearing, 1)])
    cols = lax.dynamic_slice_in_dim(cols, place * span, span, axis=1).T
    far = list(range(parts // 2, parts))[::-1]
    near = list(range(1, parts // 2))
    rotations, sums = plan(modes, slices, span)
    ready, sent, total = [], [], None

    def turn(after):
        tile, c_low, c_count, j_cuts, step = rotations.pop(0)
        tensor = phi if after is None else lax.optimization_barrier((phi, after))[0]
        ready.extend(rotate(tensor, eigvecs, pair_index, parts, tile, c_low, c_count, j_cuts, step))

    turn(None)
    for step, blocks in enumerate(ready):
        got = {0: blocks[0]}
        for s in far + near:
            block = blocks[s]
            if step > 0:
                before = [sent[-1][r] for r in (far if s == 1 else [s])]
                block, _ = lax.optimization_barrier((block, before))
            got[s] = swap(block, "mode", parts, s)
        sent.append(got)
        if rotations:
            turn(got[1])
        while sums and max(block for block, _ in sums[0][-1]) <= step:
            tile, j_low, j_count, used = sums.pop(0)
            arrived = [[sent[block][s] for block, _ in used] for s in range(parts)]
            offsets = [offset for _, offset in used]
            total = gram(arrived, offsets, three, rows, cols, probes, total, tile, j_low, j_count, 16 if j_count % 16 == 0 and j_low % 16 == 0 else 8)
    keep, give = total
    blocks = to_pairs(keep, swap(give, "mode", parts, 1), pairs)
    blocks = [b if s == 0 else swap(b, "pair", pairs, s) for s, b in enumerate(blocks)]
    blocks = to_modes(blocks, parts // 2)
    blocks = [b if s == 0 else swap(b, "mode", parts, 2 * s) for s, b in list(enumerate(blocks))[::-1]]
    local = jnp.transpose(sum(blocks), (1, 0, 2))
    row_count, _, col_count = local.shape
    row_ids = place * row_count + jnp.arange(row_count, dtype=jnp.int32)
    col_ids = lax.axis_index("pair") * col_count + jnp.arange(col_count, dtype=jnp.int32)
    offdiag = (row_ids[:, None] != col_ids[None, :]).astype(F32)
    scale = 1.0 / (modes * math.sqrt(pairs))
    return local * offdiag[:, None, :] * scale


def shards_plain(phi, eigvecs, freqs, occupations, smearing, probes, pair_index):
    tensor = phi[0]
    slices = tensor.shape[0]
    modes = tensor.shape[1]
    q_one = pair_index[0, 0]
    q_two = pair_index[0, 1]
    q_three = pair_index[0, 2]
    e_one = lax.dynamic_index_in_dim(eigvecs, q_one, 0, keepdims=False)
    e_two = lax.dynamic_index_in_dim(eigvecs, q_two, 0, keepdims=False)
    e_three = lax.dynamic_index_in_dim(eigvecs, q_three, 0, keepdims=False)
    first = jnp.dot(
        tensor.reshape(slices * modes, modes), e_one, preferred_element_type=jnp.float32
    )
    first = first.astype(jnp.bfloat16).reshape(slices, modes, modes)
    second = jnp.einsum("cbi,bj->cji", first, e_two, preferred_element_type=jnp.float32).astype(
        jnp.bfloat16
    )
    arrived = lax.all_to_all(second, "mode", split_axis=1, concat_axis=0, tiled=True)
    span = arrived.shape[1]
    count = arrived.shape[2]
    flat = lax.dot_general(
        e_three,
        arrived.reshape(arrived.shape[0], span * count),
        (((0,), (0,)), ((), ())),
        preferred_element_type=jnp.float32,
    )
    rotated = flat.astype(jnp.bfloat16).reshape(modes, span, count)
    span = rotated.shape[1]
    offset = lax.axis_index("mode") * span
    f_two = lax.dynamic_slice_in_dim(freqs[q_two], offset, span)
    n_two = lax.dynamic_slice_in_dim(occupations[q_two], offset, span)
    h_two = lax.dynamic_slice_in_dim(smearing[q_two], offset, span)
    wgt = weights(freqs[q_one], occupations[q_one], smearing[q_one], f_two, n_two, h_two, probes[0])
    flat_rot = rotated.reshape(modes, span * modes)
    weighted = (wgt.reshape(2, 1, span * modes) * flat_rot.astype(jnp.float32)[None]).astype(
        jnp.bfloat16
    )
    pair_size = lax.axis_size("pair")
    whole = jnp.einsum("wkl,nl->kwn", weighted, flat_rot, preferred_element_type=jnp.float32)
    reduced = lax.psum_scatter(whole, "pair", scatter_dimension=2, tiled=True)
    local = lax.psum_scatter(reduced, "mode", scatter_dimension=0, tiled=True)
    row_count = local.shape[0]
    col_count = local.shape[2]
    row_ids = lax.axis_index("mode") * row_count + jnp.arange(row_count, dtype=jnp.int32)
    col_ids = lax.axis_index("pair") * col_count + jnp.arange(col_count, dtype=jnp.int32)
    offdiag = (row_ids[:, None] != col_ids[None, :]).astype(jnp.float32)
    scale = 1.0 / (modes * math.sqrt(pair_size))
    return local * offdiag[:, None, :] * scale


def solution(mesh):
    pairs, parts = mesh.shape["pair"], mesh.shape["mode"]

    def either(phi, *rest):
        _, slices, modes, _ = phi.shape
        fits = slices % ROWS == 0 and modes % LANES == 0 and slices * parts == modes
        fits = fits and parts > 3 and parts & (parts - 1) == 0 and pairs & (pairs - 1) == 0
        fits = fits and modes % (8 * pairs) == 0 and modes // parts % ROWS == 0
        return (shards if fits else shards_plain)(phi, *rest)

    return jax.shard_map(
        either,
        mesh=mesh,
        in_specs=(
            P("pair", "mode", None, None),
            P(),
            P(),
            P(),
            P(),
            P("pair", None),
            P("pair", None),
        ),
        out_specs=P("mode", None, "pair"),
        check_vma=False,
    )
```
